32 devices in a mesh: fsdp: 16 (over z, y, x), seq: 2 (over core).
Axes of the slice: x: 2, y: 2, z: 4, core: 2. Of those that a mesh axis runs over, the one named last changes fastest.
Arguments:
- latents: bfloat16 [16, 256, 768], P('fsdp', 'seq'), may hold values from -6 to 6
- time_ids: int32 [16], P('fsdp'), may hold values from 0 to 1023
- class_ids: int32 [16], P('fsdp'), may hold values from 0 to 1023
- time_table: bfloat16 [1024, 768], P(('fsdp', 'seq')), may hold values from -6 to 6
- class_table: bfloat16 [1024, 768], P(('fsdp', 'seq')), may hold values from -6 to 6
- ada_w: bfloat16 [768, 4608], P(('fsdp', 'seq')), may hold values from -0.21875 to 0.21875
- ada_b: bfloat16 [4608], P(('fsdp', 'seq')), may hold values from -3 to 3
- qkv_w: bfloat16 [768, 2304], P(('fsdp', 'seq')), may hold values from -0.21875 to 0.21875
- qv_b: bfloat16 [1536], P(('fsdp', 'seq')), may hold values from -3 to 3
- proj_w: bfloat16 [768, 768], P(('fsdp', 'seq')), may hold values from -0.625 to 0.625
- proj_b: bfloat16 [768], P(('fsdp', 'seq')), may hold values from -3 to 3
- first_feedforward_weight: bfloat16 [768, 3072], P(('fsdp', 'seq')), may hold values from -0.21875 to 0.21875
- first_feedforward_bias: bfloat16 [3072], P(('fsdp', 'seq')), may hold values from -3 to 3
- second_feedforward_weight: bfloat16 [3072, 768], P(('fsdp', 'seq')), may hold values from -0.109375 to 0.109375
- second_feedforward_bias: bfloat16 [768], P(('fsdp', 'seq')), may hold values from -3 to 3
- cotangent: bfloat16 [16, 256, 768], P('fsdp', 'seq'), may hold values from -6 to 6
Outputs:
- output: bfloat16 [16, 256, 768], P('fsdp', 'seq')
- latents_grad: float32 [16, 256, 768], P('fsdp', 'seq')
- time_table_grad: float32 [1024, 768], P(('fsdp', 'seq'))
- class_table_grad: float32 [1024, 768], P(('fsdp', 'seq'))
- ada_w_grad: float32 [768, 4608], P(('fsdp', 'seq'))
- ada_b_grad: float32 [4608], P(('fsdp', 'seq'))
- qkv_w_grad: float32 [768, 2304], P(('fsdp', 'seq'))
- qv_b_grad: float32 [1536], P(('fsdp', 'seq'))
- proj_w_grad: float32 [768, 768], P(('fsdp', 'seq'))
- proj_b_grad: float32 [768], P(('fsdp', 'seq'))
- fc1_w_grad: float32 [768, 3072], P(('fsdp', 'seq'))
- fc1_b_grad: float32 [3072], P(('fsdp', 'seq'))
- fc2_w_grad: float32 [3072, 768], P(('fsdp', 'seq'))
- fc2_b_grad: float32 [768], P(('fsdp', 'seq'))
The draws below stay inside these ranges and needn't reach their ends.
All inputs are finite; a program needn't handle non-finite values.
Results may differ from the reference program's by a relative error of at most 0.028.
Values may be sent and summed in bfloat16 or wider, within the bound.
No kernel may reach another device: no remote copies, remote signals or barrier semaphores. Data moves between devices by JAX's collectives and lax.ppermute only.
A program may use at most 192 MiB of HBM per device.

```python
import jax
import jax.numpy as jnp
from jax import lax

D = 768
HD = 64
FF = 3072
STEPS = 1024
CLASSES = 1024
SEQLEN = 256
BATCH = 16


def place_ends(drawn, own_key, low, largest):
    place = [jax.random.randint(jax.random.fold_in(own_key, axis), (), 0, length) for axis, length in enumerate(drawn.shape)]
    main_axis = drawn.shape.index(max(drawn.shape))
    beside = place[:main_axis] + [(place[main_axis] + 1) % drawn.shape[main_axis]] + place[main_axis + 1:]
    return drawn.at[tuple(place)].set(low).at[tuple(beside)].set(largest)


def shard_levels(key, dims, cuts, least, top_value):
    def one(dim, blocks):
        draws = jax.random.uniform(jax.random.fold_in(jax.random.fold_in(key, 6), dim), (blocks,), jnp.float32, least / len(cuts), top_value / len(cuts))
        return jnp.repeat(jnp.exp(draws), dims[dim] // blocks).reshape((-1,) + (1,) * (len(dims) - dim - 1))

    loudness = one(*cuts[0])
    for cut in cuts[1:]:
        loudness = loudness * one(*cut)
    return loudness


def centred(rng, shape, width, limit, pieces=(), dtype=jnp.bfloat16):
    loudness = shard_levels(rng, shape, pieces, -0.22, 0.18) if pieces else 1.0
    entries = jax.random.normal(rng, shape, jnp.float32) * width * loudness
    return jnp.minimum(jnp.maximum(entries, -limit), limit).astype(dtype)


def setup_inputs(seed: int = 0) -> dict:
    key_of = jax.random.split(jax.random.key(seed), 17)
    return {
        "latents": centred(key_of[0], (BATCH, SEQLEN, D), 1.0, 6.0, ((0, 16), (1, 2))),
        "time_ids": place_ends(jax.random.randint(key_of[1], (BATCH,), 0, STEPS), jax.random.fold_in(key_of[1], 1), 0, STEPS - 1).astype(jnp.int32),
        "class_ids": place_ends(jax.random.randint(key_of[2], (BATCH,), 0, CLASSES), jax.random.fold_in(key_of[2], 1), 0, CLASSES - 1).astype(jnp.int32),
        "time_table": centred(key_of[3], (STEPS, D), 1.0, 6.0, ((0, 32),)),
        "class_table": centred(key_of[4], (CLASSES, D), 1.0, 6.0, ((0, 32),)),
        "ada_w": centred(key_of[5], (D, 6 * D), D ** -0.5, 0.21875, ((0, 32),)),
        "ada_b": centred(key_of[6], (6 * D,), 0.5, 3.0, ((0, 32),)),
        "qkv_w": centred(key_of[7], (D, 3 * D), D ** -0.5, 0.21875, ((0, 32),)),
        "qv_b": centred(key_of[8], (2 * D,), 0.5, 3.0, ((0, 32),)),
        "proj_w": centred(key_of[9], (D, D), (D // 8) ** -0.5, 0.625, ((0, 32),)),
        "proj_b": centred(key_of[10], (D,), 0.5, 3.0, ((0, 32),)),
        "first_feedforward_weight": centred(key_of[11], (D, FF), D ** -0.5, 0.21875, ((0, 32),)),
        "first_feedforward_bias": centred(key_of[12], (FF,), 0.5, 3.0, ((0, 32),)),
        "second_feedforward_weight": centred(key_of[13], (FF, D), FF ** -0.5, 0.109375, ((0, 32),)),
        "second_feedforward_bias": centred(key_of[14], (D,), 0.5, 3.0, ((0, 32),)),
        "cotangent": centred(key_of[15], (BATCH, SEQLEN, D), 1.0, 6.0, ((0, 16), (1, 2))),
    }


norm_eps = 1e-06
highest = lax.Precision.HIGHEST

def layer_norm(stream):
    center = stream - lax.optimization_barrier(jnp.mean(stream, -1, keepdims=True))
    spread = lax.optimization_barrier(jnp.mean(center * center, -1, keepdims=True))
    return center * lax.rsqrt(spread + norm_eps)

def modulate(stream, shift_part, scale_part):
    return layer_norm(stream) * (1.0 + scale_part) + shift_part

def gelu_tanh(preactivation_values):
    return jax.nn.gelu(preactivation_values, approximate=True)

def weighted_product(form, left, right):
    return jnp.einsum(form, left.astype(jnp.float32), right.astype(jnp.float32), precision=highest)

def split_heads(tensor):
    return tensor.reshape(tensor.shape[0], tensor.shape[1], tensor.shape[2] // HD, HD)

def one_group(latents, cotangent, time_ids, class_ids, params):
    time_table, class_table, ada_w, ada_b, qkv_w, qv_b, proj_w, proj_b, first_feedforward_weight, first_feedforward_bias, second_feedforward_weight, second_feedforward_bias = params
    features = latents.shape[2]
    root_inv = HD ** (-0.5)
    embedded = time_table[time_ids].astype(jnp.float32) + class_table[class_ids].astype(jnp.float32)
    condition = jax.nn.silu(embedded).astype(jnp.bfloat16)
    modulation = jnp.dot(condition, ada_w, preferred_element_type=jnp.float32) + ada_b.astype(jnp.float32)
    blocks = [modulation[:, None, index * features:(index + 1) * features] for index in range(6)]
    shift_first, scale_first, gate_first, shift_second, scale_second, gate_second = blocks
    stream = latents.astype(jnp.float32)
    normed_first = modulate(stream, shift_first, scale_first).astype(jnp.bfloat16)
    qkv_out = weighted_product('lsd,de->lse', normed_first, qkv_w)
    queries = (qkv_out[..., :features] + qv_b[:features].astype(jnp.float32)).astype(jnp.bfloat16)
    keys_all = qkv_out[..., features:2 * features].astype(jnp.bfloat16)
    values_all = (qkv_out[..., 2 * features:] + qv_b[features:].astype(jnp.float32)).astype(jnp.bfloat16)
    q_heads = split_heads(queries)
    k_heads = split_heads(keys_all)
    v_heads = split_heads(values_all)
    scores = weighted_product('lqhd,lkhd->lhqk', q_heads, k_heads) * root_inv
    row_max = lax.optimization_barrier(jnp.max(scores, -1, keepdims=True))
    log_total = row_max + jnp.log(lax.optimization_barrier(jnp.sum(jnp.exp(scores - row_max), -1, keepdims=True)))
    exact = jnp.exp(scores - log_total)
    probs = exact.astype(jnp.bfloat16)
    attended = weighted_product('lhqk,lkhd->lqhd', probs, v_heads).reshape(latents.shape).astype(jnp.bfloat16)
    branch = weighted_product('lsd,de->lse', attended, proj_w) + proj_b.astype(jnp.float32)
    residual = stream + gate_first * branch
    second_normed_input = modulate(residual, shift_second, scale_second).astype(jnp.bfloat16)
    preactivation_values = weighted_product('zxw,wh->zxh', second_normed_input, first_feedforward_weight) + first_feedforward_bias.astype(jnp.float32)
    gelu_activation = gelu_tanh(preactivation_values).astype(jnp.bfloat16)
    feedforward_output = weighted_product('yxt,ti->yxi', gelu_activation, second_feedforward_weight) + second_feedforward_bias.astype(jnp.float32)
    output = (residual + gate_second * feedforward_output).astype(jnp.bfloat16)
    upstream = cotangent.astype(jnp.float32)
    d_gate_second = lax.optimization_barrier(jnp.sum(upstream * feedforward_output, 1))
    feedforward_gradient = (upstream * gate_second).astype(jnp.bfloat16)
    second_feedforward_gradient = weighted_product('avr,avm->rm', gelu_activation, feedforward_gradient)
    fc2_bias_grad = lax.optimization_barrier(jnp.sum(feedforward_gradient.astype(jnp.float32), (0, 1)))
    activation_gradient = weighted_product('pqh,ah->pqa', feedforward_gradient, second_feedforward_weight)
    preactivation_gradient = jax.vjp(gelu_tanh, preactivation_values)[1](activation_gradient)[0].astype(jnp.bfloat16)
    first_feedforward_gradient = weighted_product('ryk,ryt->kt', second_normed_input, preactivation_gradient)
    fc1_bias_grad = lax.optimization_barrier(jnp.sum(preactivation_gradient.astype(jnp.float32), (0, 1)))
    second_normed_gradient = weighted_product('jmv,yv->jmy', preactivation_gradient, first_feedforward_weight)
    back_second = jax.vjp(modulate, residual, shift_second, scale_second)[1](second_normed_gradient)
    d_residual = upstream + back_second[0]
    d_gate_first = lax.optimization_barrier(jnp.sum(d_residual * branch, 1))
    d_branch = (d_residual * gate_first).astype(jnp.bfloat16)
    proj_grad = weighted_product('lsd,lse->de', attended, d_branch)
    proj_bias_grad = lax.optimization_barrier(jnp.sum(d_branch.astype(jnp.float32), (0, 1)))
    d_attended = weighted_product('lse,de->lsd', d_branch, proj_w).astype(jnp.bfloat16)
    do_heads = split_heads(d_attended)
    d_values = weighted_product('lhqk,lqhd->lkhd', probs, do_heads)
    d_probs = weighted_product('lqhd,lkhd->lhqk', do_heads, v_heads)
    delta = weighted_product('lqhd,lqhd->lhq', do_heads, split_heads(attended))
    d_scores = (exact * (d_probs - delta[..., None]) * root_inv).astype(jnp.bfloat16)
    d_queries = weighted_product('lhqk,lkhd->lqhd', d_scores, k_heads).reshape(latents.shape)
    d_keys = weighted_product('lhqk,lqhd->lkhd', d_scores, q_heads).reshape(latents.shape)
    d_qkv = jnp.concatenate([d_queries, d_keys, d_values.reshape(latents.shape)], -1).astype(jnp.bfloat16)
    qkv_grad = weighted_product('lsd,lse->de', normed_first, d_qkv)
    d_qkv_wide = d_qkv.astype(jnp.float32)
    qv_bias_grad = jnp.concatenate([lax.optimization_barrier(jnp.sum(d_qkv_wide[..., :features], (0, 1))), lax.optimization_barrier(jnp.sum(d_qkv_wide[..., 2 * features:], (0, 1)))])
    d_normed_first = weighted_product('lse,de->lsd', d_qkv, qkv_w)
    back_first = jax.vjp(modulate, stream, shift_first, scale_first)[1](d_normed_first)
    latents_grad = d_residual + back_first[0]
    d_modulation = jnp.concatenate([back_first[1][:, 0], back_first[2][:, 0], d_gate_first, back_second[1][:, 0], back_second[2][:, 0], d_gate_second], -1)
    ada_grad = jnp.dot(condition.astype(jnp.float32).T, d_modulation, precision=highest)
    ada_bias_grad = lax.optimization_barrier(jnp.sum(d_modulation, 0))
    d_condition = jnp.dot(d_modulation, ada_w.astype(jnp.float32).T, precision=highest)
    d_embedded = jax.vjp(jax.nn.silu, embedded)[1](d_condition)[0]
    time_grad = jnp.zeros(time_table.shape, jnp.float32).at[time_ids].add(d_embedded)
    class_grad = jnp.zeros(class_table.shape, jnp.float32).at[class_ids].add(d_embedded)
    grads = (time_grad, class_grad, ada_grad, ada_bias_grad, qkv_grad, qv_bias_grad, proj_grad, proj_bias_grad, first_feedforward_gradient, fc1_bias_grad, second_feedforward_gradient, fc2_bias_grad)
    return (output, latents_grad, grads)

def reference(latents, time_ids, class_ids, time_table, class_table, ada_w, ada_b, qkv_w, qv_b, proj_w, proj_b, first_feedforward_weight, first_feedforward_bias, second_feedforward_weight, second_feedforward_bias, cotangent):
    params = (time_table, class_table, ada_w, ada_b, qkv_w, qv_b, proj_w, proj_b, first_feedforward_weight, first_feedforward_bias, second_feedforward_weight, second_feedforward_bias)
    block_count = latents.shape[0] // 16
    lat_blocks = latents.reshape(block_count, 16, latents.shape[1], latents.shape[2])
    cot_blocks = cotangent.reshape(lat_blocks.shape)
    time_blocks = time_ids.reshape(block_count, 16)
    class_blocks = class_ids.reshape(block_count, 16)
    initial = tuple((jnp.zeros(param.shape, jnp.float32) for param in params))

    def advance(carry, items):
        output, latents_grad, grads = one_group(items[0], items[1], items[2], items[3], params)
        return (tuple((total + grad for total, grad in zip(carry, grads))), (output, latents_grad))
    totals, (outputs, input_grads) = lax.scan(advance, initial, (lat_blocks, cot_blocks, time_blocks, class_blocks))
    return (outputs.reshape(latents.shape), input_grads.reshape(latents.shape), totals[0], totals[1], totals[2], totals[3], totals[4], totals[5], totals[6], totals[7], totals[8], totals[9], totals[10], totals[11])
```

```python
import functools

import jax
import jax.numpy as jnp
from jax import lax
from jax.experimental import pallas as pl
from jax.experimental.pallas import tpu as pltpu
from jax.sharding import PartitionSpec as P

HD = 64
norm_eps = 1e-06
highest = lax.Precision.HIGHEST
f32 = jnp.float32
bf16 = jnp.bfloat16
BOTH = ("fsdp", "seq")


def layer_norm(stream):
    center = stream - jnp.mean(stream, -1, keepdims=True)
    spread = jnp.mean(center * center, -1, keepdims=True)
    return center * lax.rsqrt(spread + norm_eps)


def modulate(stream, shift_part, scale_part):
    return layer_norm(stream) * (1.0 + scale_part) + shift_part


def gelu_tanh(values):
    return jax.nn.gelu(values, approximate=True)


def dot(a, b, out=f32):
    return jnp.dot(a, b, preferred_element_type=f32).astype(out)


def dot_t(a, b, out=f32):
    return lax.dot_general(a, b, (((0,), (0,)), ((), ())), preferred_element_type=f32).astype(out)


def dot_nt(a, b, out=f32):
    return lax.dot_general(a, b, (((1,), (1,)), ((), ())), preferred_element_type=f32).astype(out)


class Chips:
    def __init__(self, count):
        self.count = count
        self.bits = count.bit_length() - 1
        assert count == 1 << self.bits and self.bits >= 2
        outer = list(range(2, self.bits))
        self.orders = (outer + [0, 1], outer + [1, 0])

    def step(self, x, k):
        pairs = [
            (2 * i + core, 2 * (i ^ (1 << self.orders[core][k])) + core)
            for i in range(self.count)
            for core in range(2)
        ]
        return lax.ppermute(x, BOTH, pairs)

    def flips(self, core):
        order = self.orders[core]
        return [
            sum(1 << order[k] for k in range(self.bits) if (r >> k) & 1) for r in range(self.count)
        ]

    def places(self):
        me, core = lax.axis_index("fsdp"), lax.axis_index("seq")
        return [
            jnp.bitwise_xor(me, jnp.where(core == 0, a, b))
            for a, b in zip(self.flips(0), self.flips(1))
        ]

    def gather(self, block):
        held = block[None]
        for k in range(self.bits - 1):
            held = jnp.concatenate([held, self.step(held, k)], 0)
        return place(self, [held, self.step(held, self.bits - 1)])

    def scatter(self, blocks):
        half = self.count // 2
        recv = self.step(blocks[half:], self.bits - 1)
        total = blocks[:half].astype(f32) + recv.astype(f32)
        for k in range(self.bits - 2, -1, -1):
            half //= 2
            recv = self.step(total[half:].astype(bf16), k)
            total = total[:half] + recv.astype(f32)
        return total[0]


def place_kernel(chips, inward, widths, *refs):
    out = refs[-1]
    ins = refs[:-1]
    half = chips.count // 2
    for r, chip in enumerate(chips.places()):
        if inward:
            out[chip] = ins[r // half][r % half]
        else:
            start = 0
            for ref, w in zip(ins, widths):
                out[r, :, start : start + w] = ref[chip]
                start += w


def place(chips, halves):
    _, rows, columns = halves[0].shape
    if rows % 16 or columns % 128:
        held = jnp.concatenate(halves, 0)
        me, core = lax.axis_index("fsdp"), lax.axis_index("seq")
        inverse = []
        for c in range(2):
            flips = chips.flips(c)
            inverse.append(jnp.array([flips.index(x) for x in range(chips.count)], jnp.int32))
        table = jnp.where(core == 0, inverse[0], inverse[1])
        return held[table[jnp.bitwise_xor(me, jnp.arange(chips.count))]]
    return pl.pallas_call(
        functools.partial(place_kernel, chips, True, None),
        out_shape=jax.ShapeDtypeStruct((chips.count, rows, columns), halves[0].dtype),
        in_specs=[pl.BlockSpec(memory_space=pltpu.VMEM)] * 2,
        out_specs=pl.BlockSpec(memory_space=pltpu.VMEM),
        compiler_params=pltpu.CompilerParams(vmem_limit_bytes=32 << 20),
        name="place",
    )(*halves)


def relative(chips, arrays):
    rows = arrays[0].shape[1]
    widths = [a.shape[2] for a in arrays]
    if rows % 16 or any(w % 128 for w in widths):
        return jnp.concatenate(arrays, 2)[jnp.stack(chips.places())]
    return pl.pallas_call(
        functools.partial(place_kernel, chips, False, widths),
        out_shape=jax.ShapeDtypeStruct((chips.count, rows, sum(widths)), arrays[0].dtype),
        in_specs=[pl.BlockSpec(memory_space=pltpu.VMEM)] * len(arrays),
        out_specs=pl.BlockSpec(memory_space=pltpu.VMEM),
        compiler_params=pltpu.CompilerParams(vmem_limit_bytes=32 << 20),
        name="relative",
    )(*arrays)


def other_core(x):
    return lax.ppermute(x, "seq", [(0, 1), (1, 0)])


def shards(
    chips,
    latents,
    time_ids,
    class_ids,
    time_table,
    class_table,
    ada_w,
    ada_b,
    qkv_w,
    qv_b,
    proj_w,
    proj_b,
    fc1_w,
    fc1_b,
    fc2_w,
    fc2_b,
    cotangent,
):
    n = chips.count
    nd = 2 * n
    me, core = lax.axis_index("fsdp"), lax.axis_index("seq")
    first = core == 0
    own_tokens, D = latents.shape[1:]
    half = D // 2
    FF = fc1_w.shape[1]
    rows = qkv_w.shape[0]
    ff_rows = fc2_w.shape[0]
    table_rows = time_table.shape[0]
    root_inv = HD ** (-0.5)

    def pick(pair):
        return jnp.where(first, pair[0], pair[1]), jnp.where(first, pair[1], pair[0])

    def in_order(mine, others, axis):
        a, b = pick((mine, others))
        return jnp.concatenate([a, b], axis)

    qkv_parts = qkv_w.reshape(rows, 3, 2, half)
    qkv_mine, qkv_others = pick((qkv_parts[:, :, 0], qkv_parts[:, :, 1]))
    proj_mine, proj_others = pick((proj_w[:, :half], proj_w[:, half:]))
    fc1_parts = fc1_w.reshape(rows, n, 2, ff_rows)
    fc1_mine, fc1_others = pick((fc1_parts[:, :, 0], fc1_parts[:, :, 1]))

    def across(mine, others):
        return in_order(mine, other_core(others), 0)

    block_q = across(
        jnp.concatenate([qkv_mine.reshape(rows, 3 * half), proj_mine], 1),
        jnp.concatenate([qkv_others.reshape(rows, 3 * half), proj_others], 1),
    )
    tokens = jnp.concatenate([latents, cotangent], 0)
    tokens = jnp.concatenate([tokens, other_core(tokens)], 1)
    stream = tokens[0].astype(f32)
    upstream = tokens[1].astype(f32)

    width = 2 * table_rows
    cols = D // nd
    table = jnp.concatenate([time_table, class_table], 0).T.reshape(nd, cols, width)
    ids = jnp.stack([time_ids[0], class_ids[0]])
    extras = jnp.concatenate(
        [fc1_b, qv_b, proj_b, fc2_b, ada_b, (ids // 32).astype(bf16), (ids % 32).astype(bf16)]
    )
    extra_count = extras.shape[0]
    extra_rows = -(-extra_count // width)
    extras = jnp.pad(extras, (0, extra_rows * width - extra_count)).reshape(1, extra_rows, width)
    sent = jnp.concatenate([table, jnp.broadcast_to(extras, (nd, extra_rows, width))], 1)
    got = lax.all_to_all(sent, BOTH, 0, 0, tiled=True)
    extras = got[:, cols:].reshape(nd, extra_rows * width)
    bounds = [0]
    for b in (fc1_b, qv_b, proj_b, fc2_b, ada_b):
        bounds.append(bounds[-1] + b.shape[0])
    fc1_bias, qv_bias, proj_bias, fc2_bias, ada_bias = (
        extras[:, a:b].astype(f32) for a, b in zip(bounds[:-1], bounds[1:])
    )
    fc1_bias = fc1_bias.reshape(n, 2, ff_rows)
    fc1_bias = pick((fc1_bias[:, 0], fc1_bias[:, 1]))[0].reshape(n * ff_rows)
    qv_bias = qv_bias.reshape(2, 2, half)
    qv_bias = pick((qv_bias[:, 0], qv_bias[:, 1]))[0]
    id_parts = extras[::2, bounds[-1] : bounds[-1] + 4].astype(jnp.int32)
    all_ids = id_parts[:, :2] * 32 + id_parts[:, 2:]

    def hot(which, base):
        rows_of = base + lax.broadcasted_iota(jnp.int32, (nd, table_rows, n), 1)
        return (all_ids[:, which][None, None] == rows_of).astype(bf16)

    base = lax.broadcasted_iota(jnp.int32, (nd, table_rows, n), 0) * table_rows
    hot_both = jnp.concatenate([hot(0, base), hot(1, base)], 1)
    embedded = jnp.einsum("sdr,srl->ld", got[:, :cols], hot_both, preferred_element_type=f32)
    condition = jax.nn.silu(embedded).astype(bf16)
    partial = dot(condition, ada_w)
    lanes = 128 if (6 * D) % 128 == 0 else 6 * D
    partial = lax.all_to_all(partial.reshape(n, 6 * D // lanes, lanes), "fsdp", 0, 0, tiled=True)
    modulation = jnp.sum(partial, 0)
    modulation = (modulation + other_core(modulation)).reshape(6 * D) + ada_bias.reshape(6 * D)
    shift_first, scale_first, gate_first, shift_second, scale_second, gate_second = (
        modulation[None, i * D : (i + 1) * D] for i in range(6)
    )

    weights_q = chips.gather(block_q)
    qkv_full = weights_q[:, :, : 3 * half].reshape(D, 3 * half)
    proj_cols = weights_q[:, :, 3 * half :].reshape(2, half, half)
    block_1 = across(fc1_mine.reshape(rows, FF // 2), fc1_others.reshape(rows, FF // 2))
    fc1_full = chips.gather(block_1).reshape(D, FF // 2)
    fc2_full = chips.gather(fc2_w).reshape(FF // 2, D)
    proj_rows_mine, proj_rows_others = pick((proj_cols[0], proj_cols[1]))
    proj_full = in_order(proj_rows_mine, other_core(proj_rows_others), 1)

    normed_first = modulate(stream, shift_first, scale_first).astype(bf16)
    qkv_out = dot(normed_first, qkv_full)
    queries = (qkv_out[:, :half] + qv_bias[0]).astype(bf16)
    keys = qkv_out[:, half : 2 * half].astype(bf16)
    values = (qkv_out[:, 2 * half :] + qv_bias[1]).astype(bf16)

    def heads(x):
        return x.reshape(x.shape[0], half // HD, HD)

    q_heads, k_heads, v_heads = heads(queries), heads(keys), heads(values)
    scores = jnp.einsum("qhd,khd->hqk", q_heads, k_heads, preferred_element_type=f32) * root_inv
    row_max = jnp.max(scores, -1, keepdims=True)
    log_total = row_max + jnp.log(jnp.sum(jnp.exp(scores - row_max), -1, keepdims=True))
    exact = jnp.exp(scores - log_total)
    probs = exact.astype(bf16)
    attended = jnp.einsum("hqk,khd->qhd", probs, v_heads, preferred_element_type=f32)
    attended = attended.reshape(stream.shape[0], half).astype(bf16)

    def summed(x):
        got = other_core(x)
        return x + jnp.concatenate([got[own_tokens:], got[:own_tokens]], 0)

    branch = summed(dot(attended, proj_full)) + proj_bias.reshape(D)
    residual = stream + gate_first * branch
    normed_second = modulate(residual, shift_second, scale_second).astype(bf16)
    pre_act = dot(normed_second, fc1_full) + fc1_bias
    activated = gelu_tanh(pre_act).astype(bf16)
    mlp_part = dot(activated, fc2_full)
    mlp_own = mlp_part[:own_tokens] + other_core(mlp_part[own_tokens:]) + fc2_bias.reshape(D)
    output = (residual[:own_tokens] + gate_second * mlp_own).astype(bf16)

    d_gate_second = jnp.sum(upstream[:own_tokens] * mlp_own, 0)
    d_mlp = (upstream * gate_second).astype(bf16)
    fc2_grad = dot_t(activated, d_mlp, bf16).reshape(n, ff_rows, D)
    fc2_grad = chips.scatter(relative(chips, [fc2_grad]))
    fc2_b_grad = jnp.sum(d_mlp[:own_tokens].astype(f32), 0)
    d_act = dot_nt(d_mlp, fc2_full)
    d_pre = jax.vjp(gelu_tanh, pre_act)[1](d_act)[0].astype(bf16)
    fc1_grad = dot_t(normed_second, d_pre, bf16).reshape(n, 2 * rows, FF // 2)
    fc1_b_grad = jnp.sum(d_pre.astype(f32), 0)
    d_normed_second = summed(dot_nt(d_pre, fc1_full))
    back_second = jax.vjp(lambda v: modulate(v, shift_second, scale_second), residual)[1](
        d_normed_second
    )[0]
    d_residual = upstream + back_second
    own_normed = d_normed_second[:own_tokens]
    d_shift_second = jnp.sum(own_normed, 0)
    d_scale_second = jnp.sum(own_normed * layer_norm(residual[:own_tokens]), 0)
    d_gate_first = jnp.sum(d_residual[:own_tokens] * branch[:own_tokens], 0)
    d_branch = (d_residual * gate_first).astype(bf16)
    proj_b_grad = jnp.sum(d_branch[:own_tokens].astype(f32), 0)
    proj_grad = dot_t(attended, d_branch, bf16)
    proj_g_mine, proj_g_others = pick((proj_grad[:, :half], proj_grad[:, half:]))
    proj_grad = in_order(proj_g_mine, other_core(proj_g_others), 0).reshape(n, 2 * rows, half)
    fc1_proj_grad = chips.scatter(relative(chips, [fc1_grad, proj_grad]))

    d_attended = dot_nt(d_branch, proj_full, bf16)
    do_heads = heads(d_attended)
    d_values = jnp.einsum("hqk,qhd->khd", probs, do_heads, preferred_element_type=f32)
    d_probs = jnp.einsum("qhd,khd->hqk", do_heads, v_heads, preferred_element_type=f32)
    delta = jnp.einsum("qhd,qhd->hq", do_heads, heads(attended), preferred_element_type=f32)
    d_scores = (exact * (d_probs - delta[..., None]) * root_inv).astype(bf16)
    d_queries = jnp.einsum("hqk,khd->qhd", d_scores, k_heads, preferred_element_type=f32)
    d_keys = jnp.einsum("hqk,qhd->khd", d_scores, q_heads, preferred_element_type=f32)
    d_qkv = jnp.concatenate(
        [x.reshape(x.shape[0], half).astype(bf16) for x in (d_queries, d_keys, d_values)], -1
    )
    qkv_grad = dot_t(normed_first, d_qkv, bf16).reshape(n, 2 * rows, 3 * half)
    qkv_grad = chips.scatter(relative(chips, [qkv_grad]))
    d_qkv_sum = jnp.sum(d_qkv.astype(f32), 0)
    d_normed_part = dot_nt(d_qkv, qkv_full)
    d_normed_first = d_normed_part[:own_tokens] + other_core(d_normed_part[own_tokens:])
    own_stream = stream[:own_tokens]
    back_first = jax.vjp(lambda v: modulate(v, shift_first, scale_first), own_stream)[1](
        d_normed_first
    )[0]
    latents_grad = d_residual[:own_tokens] + back_first
    d_shift_first = jnp.sum(d_normed_first, 0)
    d_scale_first = jnp.sum(d_normed_first * layer_norm(own_stream), 0)

    def by_core(x):
        zero = jnp.zeros_like(x)
        return jnp.stack([jnp.where(first, x, zero), jnp.where(first, zero, x)], 1)

    fc1_b_part = by_core(fc1_b_grad.reshape(n, ff_rows))
    qv_part = by_core(
        jnp.stack([d_qkv_sum[:half], d_qkv_sum[2 * half :]])
    )
    qv_part = qv_part.reshape(n, 2, D // n)
    d_mod = jnp.concatenate(
        [d_shift_first, d_scale_first, d_gate_first, d_shift_second, d_scale_second, d_gate_second]
    )
    bias_part = jnp.concatenate(
        [
            fc1_b_part,
            qv_part,
            proj_b_grad.reshape(n, 2, rows),
            fc2_b_grad.reshape(n, 2, rows),
        ],
        2,
    ).reshape(n, -1)
    small = jnp.concatenate([d_mod, bias_part.reshape(-1)])
    small = small + other_core(small)
    d_mod, bias_part = small[: 6 * D], small[6 * D :].reshape(n, -1)
    ada_b_grad = None
    sent = jnp.concatenate([jnp.broadcast_to(d_mod[None], (n, 6 * D)), bias_part], 1)
    got = lax.all_to_all(sent, "fsdp", 0, 0, tiled=True)
    d_modulation = got[:, : 6 * D]
    bias_sum = jnp.sum(got[:, 6 * D :], 0).reshape(2, -1)
    bias_own = pick((bias_sum[0], bias_sum[1]))[0]
    mod_sum = jnp.sum(d_modulation, 0)
    ada_b_grad = lax.dynamic_index_in_dim(
        mod_sum.reshape(nd, 6 * D // nd), 2 * me + core, 0, keepdims=False
    )
    ada_w_grad = lax.dot_general(
        condition.astype(f32), d_modulation, (((0,), (0,)), ((), ())), precision=highest
    )
    d_condition = lax.dot_general(
        ada_w.astype(f32), d_modulation, (((1,), (1,)), ((), ())), precision=highest
    )
    d_embedded = jax.vjp(jax.nn.silu, embedded.T)[1](d_condition)[0]
    d_embedded = lax.all_to_all(
        jnp.broadcast_to(d_embedded[None], (nd, cols, n)), BOTH, 0, 0, tiled=True
    ).reshape(D, n)

    def table_grad(which):
        own = (2 * me + core) * table_rows + lax.broadcasted_iota(jnp.int32, (table_rows, n), 0)
        mask = (all_ids[:, which][None] == own).astype(f32)
        return lax.dot_general(mask, d_embedded, (((1,), (1,)), ((), ())), precision=highest)

    def to_rows(grad):
        pair = grad.reshape(2, rows, grad.shape[1])
        mine, others = pick((pair[0], pair[1]))
        return pick((mine, other_core(others)))

    fp = to_rows(fc1_proj_grad)
    fc1_w_grad = jnp.stack(
        [x[:, : FF // 2].reshape(rows, n, ff_rows) for x in fp], 2
    ).reshape(rows, FF)
    proj_w_grad = jnp.concatenate([x[:, FF // 2 :] for x in fp], 1)
    qkv_w_grad = jnp.stack([x.reshape(rows, 3, half) for x in to_rows(qkv_grad)], 2).reshape(
        rows, 3 * D
    )
    a, b, c = ff_rows, ff_rows + D // n, ff_rows + D // n + rows
    return (
        output[None],
        latents_grad[None],
        table_grad(0),
        table_grad(1),
        ada_w_grad,
        ada_b_grad,
        qkv_w_grad,
        bias_own[a:b],
        proj_w_grad,
        bias_own[b:c],
        fc1_w_grad,
        bias_own[:a],
        fc2_grad,
        bias_own[c:],
    )


def solution(mesh):
    assert mesh.shape["seq"] == 2
    chips = Chips(mesh.shape["fsdp"])
    tokens = P("fsdp", "seq", None)
    matrix = P(BOTH, None)
    vector = P(BOTH)
    in_specs = (tokens, P("fsdp"), P("fsdp")) + (matrix,) * 3 + (vector, matrix) * 4 + (vector, tokens)
    in_specs = (
        tokens,
        P("fsdp"),
        P("fsdp"),
        matrix,
        matrix,
        matrix,
        vector,
        matrix,
        vector,
        matrix,
        vector,
        matrix,
        vector,
        matrix,
        vector,
        tokens,
    )
    out_specs = (
        tokens,
        tokens,
        matrix,
        matrix,
        matrix,
        vector,
        matrix,
        vector,
        matrix,
        vector,
        matrix,
        vector,
        matrix,
        vector,
    )
    return jax.shard_map(
        functools.partial(shards, chips),
        mesh=mesh,
        in_specs=in_specs,
        out_specs=out_specs,
        check_vma=False,
    )
```

```python
import functools

import jax
import jax.numpy as jnp
from jax import lax
from jax.experimental import pallas as pl
from jax.experimental.pallas import tpu as pltpu
from jax.sharding import PartitionSpec as P

HD = 64
norm_eps = 1e-06
highest = lax.Precision.HIGHEST
f32 = jnp.float32
bf16 = jnp.bfloat16
BOTH = ("fsdp", "seq")


def dot(a, b, out=f32):
    return jnp.dot(a, b, preferred_element_type=f32).astype(out)


def dot_t(a, b, out=f32):
    return lax.dot_general(a, b, (((0,), (0,)), ((), ())), preferred_element_type=f32).astype(out)


def dot_nt(a, b, out=f32):
    return lax.dot_general(a, b, (((1,), (1,)), ((), ())), preferred_element_type=f32).astype(out)


class Chips:
    def __init__(self, count):
        self.count = count
        self.ring = count // 4
        assert count == 4 * self.ring
        self.back = self.ring // 2
        self.ahead = self.ring - 1 - self.back
        self.offsets = [0]
        self.offsets += [-j for j in range(1, self.back + 1)]
        self.offsets += list(range(1, self.ahead + 1))

    def shift(self, x, by):
        pairs = [(i, (i + 4 * by) % self.count) for i in range(self.count)]
        with jax.named_scope(f"ring_by_{by % self.ring}"):
            return lax.ppermute(x, "fsdp", pairs)

    def swap(self, x, last):
        pairs = [
            (2 * i + core, 2 * (i ^ (1 << (core ^ last))) + core)
            for i in range(self.count)
            for core in range(2)
        ]
        with jax.named_scope("last_swap" if last else "first_swap"):
            return lax.ppermute(x, BOTH, pairs)

    def places(self, ring_first):
        me, core = lax.axis_index("fsdp"), lax.axis_index("seq")
        outer, inner = me // 4, me % 4
        places = []
        for r in range(self.count):
            swaps, place = (r // self.ring, r % self.ring) if ring_first else (r % 4, r // 4)
            a, b = swaps % 2, swaps // 2
            flip = jnp.where(core == 0, a + 2 * b, 2 * a + b)
            place = lax.rem(outer + self.offsets[place] + self.ring, self.ring)
            places.append(4 * place + jnp.bitwise_xor(inner, flip))
        return places

    def ring_gather(self, blocks, direct, tie=None):
        held = [blocks]
        if direct:
            return held + [self.shift(blocks, -offset) for offset in self.offsets[1:]], tie
        up, down = self.shift(blocks, 1), self.shift(blocks, -1)
        if tie is not None:
            (up, down), tie = after((up, down), tie)
        for count, by, moved in ((self.back, 1, up), (self.ahead, -1, down)):
            for j in range(count):
                moved = self.shift(moved, by) if j else moved
                held.append(moved)
        return held, tie

    def direct_scatter(self, blocks):
        return [self.shift(x.astype(bf16), o) for x, o in zip(blocks[1:], self.offsets[1:])]

    def ring_scatter(self, blocks):
        total = blocks[0].astype(f32)
        early = []
        for first, last, by in ((self.back, 1, -1), (self.ring - 1, self.back + 1, 1)):
            term = None
            for r in range(first, last - 1, -1):
                term = blocks[r] if term is None else blocks[r].astype(f32) + term
                term = self.shift(term.astype(bf16), by)
                if r == first:
                    early.append(term)
                term = term.astype(f32)
            if term is not None:
                total = total + term
        return total, early

    def swap_add(self, kept, sent, last):
        got = self.swap(sent, last)
        half = kept.shape[0] // 2
        return [
            (kept[i * half : (i + 1) * half].astype(f32) + got[i * half : (i + 1) * half].astype(f32))
            for i in range(2)
        ]


def after(x, earlier):
    return lax.optimization_barrier((x, earlier))


def turned(chips, place):
    return lax.rem(place + lax.axis_index("seq") * (chips.count // 2), chips.count)


def place_kernel(chips, ring_first, sizes, widths, *refs):
    ins, outs = refs[: len(sizes)], refs[len(sizes) :]
    places = chips.places(ring_first)
    r = 0
    for ref, size in zip(ins, sizes):
        for i in range(size):
            outs[0][places[r]] = ref[i, :, : widths[0]]
            if len(outs) > 1:
                outs[1][turned(chips, places[r])] = ref[i, :, widths[0] :]
            r += 1


def relative_kernel(chips, ring_first, count, width, *refs):
    ins, outs = refs[:-count], refs[-count:]
    size, half = chips.count // count, chips.count // 2
    for r, place in enumerate(chips.places(ring_first)):
        outs[r // size][r % size, :, :width] = ins[0][place]
        if len(ins) > 1:
            at = turned(chips, place)
            low = ins[1][jnp.minimum(at, half - 1)]
            high = ins[2][jnp.maximum(at - half, 0)]
            outs[r // size][r % size, :, width:] = jnp.where(at < half, low, high)


def kernel(body, name, outs, *args, flops=0):
    shapes = [jax.ShapeDtypeStruct(shape, dtype) for shape, dtype in outs]
    moved = sum(x.size * x.dtype.itemsize for x in (*args, *shapes))
    return pl.pallas_call(
        body,
        out_shape=shapes,
        in_specs=[pl.BlockSpec(memory_space=pltpu.VMEM)] * len(args),
        out_specs=[pl.BlockSpec(memory_space=pltpu.VMEM)] * len(shapes),
        compiler_params=pltpu.CompilerParams(vmem_limit_bytes=16 << 20),
        cost_estimate=pl.CostEstimate(flops=flops, bytes_accessed=moved, transcendentals=0),
        name=name,
    )(*args)


def place(chips, ring_first, parts, widths):
    rows = parts[0].shape[1]
    if rows % 16 or any(w % 128 for w in widths):
        held = jnp.concatenate(parts, 0)
        places = jnp.stack(chips.places(ring_first))
        outs = [jnp.zeros_like(held).at[places].set(held)[:, :, : widths[0]]]
        if len(widths) > 1:
            held = held[:, :, widths[0] :]
            outs.append(jnp.zeros_like(held).at[turned(chips, places)].set(held))
        return outs
    body = functools.partial(place_kernel, chips, ring_first, [p.shape[0] for p in parts], widths)
    outs = [((chips.count, rows, w), parts[0].dtype) for w in widths]
    return kernel(body, "place", outs, *parts)


def relative(chips, ring_first, count, arrays):
    rows, width = arrays[0].shape[1:]
    widths = [a.shape[2] for a in arrays[:2]]
    if rows % 16 or any(w % 128 for w in widths):
        places = jnp.stack(chips.places(ring_first))
        held = arrays[0][places]
        if len(arrays) > 1:
            second = jnp.concatenate(arrays[1:], 0)[turned(chips, places)]
            held = jnp.concatenate([held, second], 2)
        return jnp.split(held, count)
    body = functools.partial(relative_kernel, chips, ring_first, count, width)
    shape = (chips.count // count, rows, sum(widths))
    return kernel(body, "relative", [(shape, arrays[0].dtype)] * count, *arrays)


def tiles(length, tile, body):
    def step(i, carry):
        body(pl.ds(pl.multiple_of(i * tile, tile), tile))
        return carry

    lax.fori_loop(0, length // tile, step, 0)


def normalize(v):
    center = v - jnp.mean(v, -1, keepdims=True)
    scale = lax.rsqrt(jnp.mean(center * center, -1, keepdims=True) + norm_eps)
    return center * scale, scale


def normalize_back(g, normed, scale):
    along = jnp.mean(g * normed, -1, keepdims=True)
    return scale * (g - jnp.mean(g, -1, keepdims=True) - normed * along)


def both(part, got):
    own = part.shape[0] // 2
    return part + jnp.concatenate([got[own:], got[:own]], 0)


def attention_kernel(x_ref, mod_ref, w_ref, b_ref, normed_ref, qkv_ref, att_ref, log_ref):
    normed = normalize(x_ref[...].astype(f32))[0]
    normed_ref[...] = (normed * (1.0 + mod_ref[1:2]) + mod_ref[0:1]).astype(bf16)
    half = att_ref.shape[1]
    for j in range(3):
        part = dot(normed_ref[...], w_ref[:, half * j : half * (j + 1)])
        if j != 1:
            part = part + b_ref[j // 2 : j // 2 + 1]
        qkv_ref[:, half * j : half * (j + 1)] = part.astype(bf16)
    lanes = lax.broadcasted_iota(jnp.int32, log_ref.shape, 1)
    logs = jnp.zeros(log_ref.shape, f32)
    pair = []
    for h in range(half // HD):
        q, k, v = (qkv_ref[:, half * j + HD * h : half * j + HD * (h + 1)] for j in range(3))
        scores = dot_nt(q, k) * HD ** (-0.5)
        top = jnp.max(scores, -1, keepdims=True)
        total = top + jnp.log(jnp.sum(jnp.exp(scores - top), -1, keepdims=True))
        pair.append(dot(jnp.exp(scores - total).astype(bf16), v, bf16))
        logs = jnp.where(lanes == h, total, logs)
        if h % 2:
            att_ref[:, HD * (h - 1) : HD * (h + 1)] = jnp.concatenate(pair, 1)
            pair = []
    log_ref[...] = logs


def project_kernel(att_ref, mine_ref, other_ref, part_ref, w_ref):
    half = att_ref.shape[1]
    first = lax.axis_index("seq") == 0
    w_ref[:, :half] = jnp.where(first, mine_ref[...], other_ref[...])
    w_ref[:, half:] = jnp.where(first, other_ref[...], mine_ref[...])
    part_ref[...] = dot(att_ref[...], w_ref[...])


def mlp_kernel(
    x_ref, part_ref, got_ref, bias_ref, mod_ref, cot_ref, w_ref, b_ref,
    residual_ref, branch_ref, normed_ref, act_ref, slope_ref, d_mlp_ref, grad_ref,
):
    branch = both(part_ref[...], got_ref[...]) + bias_ref[...]
    branch_ref[...] = branch[: branch_ref.shape[0]]
    residual = x_ref[...].astype(f32) + mod_ref[2:3] * branch
    residual_ref[...] = residual
    normed = normalize(residual)[0]
    normed_ref[...] = (normed * (1.0 + mod_ref[4:5]) + mod_ref[3:4]).astype(bf16)
    d_mlp_ref[...] = (cot_ref[...].astype(f32) * mod_ref[5:6]).astype(bf16)

    def tile(cols):
        v = dot(normed_ref[...], w_ref[:, cols]) + b_ref[:, cols]
        a, c = (2.0 / 3.141592653589793) ** 0.5, 0.044715
        square = v * v
        t = jnp.tanh(a * (v + c * (square * v)))
        act = (0.5 * v * (1.0 + t)).astype(bf16)
        act_ref[:, cols] = act
        slope_ref[:, cols] = 0.5 * (1.0 + t) + 0.5 * v * (1.0 - t * t) * (a * (1.0 + 3.0 * c * square))
        grad_ref[cols, :] = dot_t(act, d_mlp_ref[...], bf16)

    tiles(w_ref.shape[1], 256, tile)


def mlp_back_kernel(d_mlp_ref, slope_ref, w2_ref, w1_ref, d_pre_ref, sum_ref, d_normed_ref):
    d_normed_ref[...] = jnp.zeros_like(d_normed_ref)

    def tile(cols):
        d_pre = (dot_nt(d_mlp_ref[...], w2_ref[cols, :]) * slope_ref[:, cols]).astype(bf16)
        d_pre_ref[:, cols] = d_pre
        sum_ref[:, cols] = jnp.sum(d_pre.astype(f32), 0, keepdims=True)
        d_normed_ref[...] += dot_nt(d_pre, w1_ref[:, cols])

    tiles(w1_ref.shape[1], 256, tile)


def mlp_grad_kernel(act_ref, w2_ref, normed_ref, d_pre_ref, own_ref, sent_ref, grad_ref):
    own = own_ref.shape[0]

    def out_tile(cols):
        out = dot(act_ref[...], w2_ref[:, cols])
        own_ref[:, cols] = out[:own]
        sent_ref[:, cols] = out[own:]

    def grad_tile(cols):
        grad_ref[:, cols] = dot_t(normed_ref[...], d_pre_ref[:, cols], bf16)

    tiles(w2_ref.shape[1], 256, out_tile)
    tiles(d_pre_ref.shape[1], 256, grad_tile)


def branch_back_kernel(
    residual_ref, part_ref, got_ref, cot_ref, mod_ref, branch_ref, att_ref, w_ref, d_mlp_ref,
    d_residual_ref, d_att_ref, mine_ref, others_ref, sums_ref,
):
    own = d_residual_ref.shape[0]
    d_normed = both(part_ref[...], got_ref[...])
    normed, scale = normalize(residual_ref[...])
    back = normalize_back(d_normed * (1.0 + mod_ref[4:5]), normed, scale)
    d_residual = cot_ref[...].astype(f32) + back
    d_residual_ref[...] = d_residual[:own]
    d_branch = (d_residual * mod_ref[2:3]).astype(bf16)
    rows = (
        d_residual[:own] * branch_ref[...],
        d_normed[:own],
        d_normed[:own] * normed[:own],
        d_branch[:own].astype(f32),
        d_mlp_ref[:own, :].astype(f32),
    )
    for i, row in enumerate(rows):
        sums_ref[i : i + 1, :] = jnp.sum(row, 0, keepdims=True)
    d_att_ref[...] = dot_nt(d_branch, w_ref[...], bf16)
    grad = dot_t(att_ref[...], d_branch, bf16)
    half = mine_ref.shape[1]
    first = lax.axis_index("seq") == 0
    mine_ref[...] = jnp.where(first, grad[:, :half], grad[:, half:])
    others_ref[...] = jnp.where(first, grad[:, half:], grad[:, :half])


def attention_back_kernel(
    qkv_ref, att_ref, d_att_ref, log_ref, w_ref, d_qkv_ref, sum_ref, own_ref, sent_ref
):
    half = att_ref.shape[1]
    own = own_ref.shape[0]
    pairs = ([], [], [])
    for h in range(half // HD):
        q, k, v = (qkv_ref[:, half * j + HD * h : half * j + HD * (h + 1)] for j in range(3))
        att, d_att = (ref[:, HD * h : HD * (h + 1)] for ref in (att_ref, d_att_ref))
        exact = jnp.exp(dot_nt(q, k) * HD ** (-0.5) - log_ref[:, h : h + 1])
        delta = jnp.sum(d_att.astype(f32) * att.astype(f32), -1, keepdims=True)
        d_scores = (exact * (dot_nt(d_att, v) - delta) * HD ** (-0.5)).astype(bf16)
        pairs[0].append(dot(d_scores, k, bf16))
        pairs[1].append(dot_t(d_scores, q, bf16))
        pairs[2].append(dot_t(exact.astype(bf16), d_att, bf16))
        if h % 2:
            for j in range(3):
                cols = slice(half * j + HD * (h - 1), half * j + HD * (h + 1))
                value = jnp.concatenate(pairs[j], 1)
                d_qkv_ref[:, cols] = value
                sum_ref[:, cols] = jnp.sum(value.astype(f32), 0, keepdims=True)
            pairs = ([], [], [])

    def tile(cols):
        out = dot_nt(d_qkv_ref[...], w_ref[cols, :])
        own_ref[:, cols] = out[:own]
        sent_ref[:, cols] = out[own:]

    for start in range(0, own_ref.shape[1], 256):
        tile(slice(start, start + 256))


def qkv_grad_kernel(normed_ref, d_qkv_ref, grad_ref):
    tiles(d_qkv_ref.shape[1], 384, lambda cols: grad_ref.__setitem__(
        (slice(None), cols), dot_t(normed_ref[...], d_qkv_ref[:, cols], bf16)
    ))


def finish_kernel(
    part_ref, got_ref, x_ref, d_residual_ref, mod_ref, mlp_ref, mlp_got_ref, bias_ref, residual_ref,
    cot_ref, sums_ref, fc1_sum_ref, qkv_sum_ref, grad_ref, out_ref, small_ref,
):
    own, D = grad_ref.shape
    half = D // 2
    d_normed = part_ref[...] + got_ref[...]
    normed, scale = normalize(x_ref[...].astype(f32))
    back = normalize_back(d_normed * (1.0 + mod_ref[1:2]), normed, scale)
    grad_ref[...] = d_residual_ref[...] + back
    mlp = mlp_ref[...] + mlp_got_ref[...] + bias_ref[...]
    out_ref[...] = (residual_ref[:own, :] + mod_ref[5:6] * mlp).astype(bf16)
    first = lax.axis_index("seq") == 0
    small_ref[...] = jnp.zeros_like(small_ref)
    small_ref[0:1, :] = jnp.sum(d_normed, 0, keepdims=True)
    small_ref[1:2, :] = jnp.sum(d_normed * normed, 0, keepdims=True)
    small_ref[2:5, :] = sums_ref[0:3, :]
    small_ref[5:6, :] = jnp.sum(cot_ref[:own, :].astype(f32) * mlp, 0, keepdims=True)
    small_ref[6:8, :] = sums_ref[3:5, :]
    for i in range(2):
        part = qkv_sum_ref[:, 2 * half * i : 2 * half * i + half]
        small_ref[8 + i : 9 + i, :half] = jnp.where(first, part, 0.0)
        small_ref[8 + i : 9 + i, half:] = jnp.where(first, 0.0, part)
    count = fc1_sum_ref.shape[1] // D
    for i in range(count):
        part = fc1_sum_ref[:, D * i : D * (i + 1)]
        small_ref[10 + i : 11 + i, :] = jnp.where(first, part, 0.0)
        small_ref[10 + count + i : 11 + count + i, :] = jnp.where(first, 0.0, part)


def modulation_back_kernel(got_ref, w_ref, cond_ref, embedded_ref, grad_ref, d_embedded_ref, sums_ref):
    got = got_ref[...].astype(f32)
    sums_ref[...] = jnp.sum(got, 0)
    D = got.shape[2]
    total = jnp.zeros(d_embedded_ref.shape, f32)
    for k in range(6):
        cols = slice(D * k, D * (k + 1))
        d_mod = got[:, k].astype(bf16)
        total += dot_nt(w_ref[:, cols], d_mod)
        grad_ref[:, cols] = dot_t(cond_ref[...], d_mod)
    e = embedded_ref[...]
    gate = 1.0 / (1.0 + jnp.exp(-e))
    d_embedded_ref[...] = total * (gate * (1.0 + e * (1.0 - gate)))


def other_core(x):
    return lax.ppermute(x, "seq", [(0, 1), (1, 0)])


def shards(
    chips,
    latents,
    time_ids,
    class_ids,
    time_table,
    class_table,
    ada_w,
    ada_b,
    qkv_w,
    qv_b,
    proj_w,
    proj_b,
    fc1_w,
    fc1_b,
    fc2_w,
    fc2_b,
    cotangent,
):
    n = chips.count
    nd = 2 * n
    me, core = lax.axis_index("fsdp"), lax.axis_index("seq")
    first = core == 0
    own_tokens, D = latents.shape[1:]
    half = D // 2
    FF = fc1_w.shape[1]
    rows = qkv_w.shape[0]
    ff_rows = fc2_w.shape[0]
    table_rows = time_table.shape[0]

    def pick(pair):
        return jnp.where(first, pair[0], pair[1]), jnp.where(first, pair[1], pair[0])

    def in_order(mine, others, axis):
        a, b = pick((mine, others))
        return jnp.concatenate([a, b], axis)

    qkv_parts = qkv_w.reshape(rows, 3, 2, half)
    qkv_mine, qkv_others = pick((qkv_parts[:, :, 0], qkv_parts[:, :, 1]))
    proj_mine, proj_others = pick((proj_w[:, :half], proj_w[:, half:]))
    fc1_parts = fc1_w.reshape(rows, n, 2, ff_rows)
    fc1_mine, fc1_others = pick((fc1_parts[:, :, 0], fc1_parts[:, :, 1]))

    def across(mine, others):
        return in_order(mine, other_core(others), 0)

    block_q = across(
        jnp.concatenate([qkv_mine.reshape(rows, 3 * half), proj_mine], 1),
        jnp.concatenate([qkv_others.reshape(rows, 3 * half), proj_others], 1),
    )
    tokens = jnp.concatenate([latents, cotangent], 0)
    tokens = jnp.concatenate([tokens, other_core(tokens)], 1)

    width = 2 * table_rows
    cols = D // nd
    table = jnp.concatenate([time_table, class_table], 0).T.reshape(nd, cols, width)
    ids = jnp.stack([time_ids[0], class_ids[0]])
    ids = jnp.concatenate([ids // 32, ids % 32]).astype(bf16)
    lines, bounds = [], [cols]
    for vector in (fc1_b, qv_b, proj_b, fc2_b, ada_b, ids):
        count = -(-vector.shape[0] // width)
        lines.append(jnp.pad(vector, (0, count * width - vector.shape[0])).reshape(count, width))
        bounds.append(bounds[-1] + count)
    extras = jnp.concatenate(lines, 0)[None]
    sent = jnp.concatenate([table, jnp.broadcast_to(extras, (nd,) + extras.shape[1:])], 1)
    sent, block_q = after(sent, block_q)
    got = lax.all_to_all(sent, BOTH, 0, 0, tiled=True)

    held_2 = fc2_w[None]
    held_2 = jnp.concatenate([held_2, chips.swap(held_2, 0)], 0)
    held_2 = jnp.concatenate([held_2, chips.swap(held_2, 1)], 0)
    ring_q = jnp.concatenate(chips.ring_gather(block_q[None], True)[0], 0)
    swap_q = chips.swap(ring_q, 0)
    got, swap_q = after(got, swap_q)

    def extra(i, length):
        part = got[:, bounds[i] : bounds[i + 1]].reshape(nd, -1)
        return part[:, :length].astype(f32)

    fc1_bias, qv_bias, proj_bias, fc2_bias, ada_bias = (
        extra(i, b.shape[0]) for i, b in enumerate((fc1_b, qv_b, proj_b, fc2_b, ada_b))
    )
    fc1_bias = fc1_bias.reshape(n, 2, ff_rows)
    fc1_bias = pick((fc1_bias[:, 0], fc1_bias[:, 1]))[0].reshape(n * ff_rows)
    qv_bias = qv_bias.reshape(2, 2, half)
    qv_bias = pick((qv_bias[:, 0], qv_bias[:, 1]))[0]
    fc1_bias, proj_bias, fc2_bias = (x.reshape(1, -1) for x in (fc1_bias, proj_bias, fc2_bias))
    ada_bias = ada_bias.reshape(6 * D)
    id_parts = extra(5, 4)[::2].astype(jnp.int32)
    all_ids = id_parts[:, :2] * 32 + id_parts[:, 2:]

    def hot(which, base):
        rows_of = base + lax.broadcasted_iota(jnp.int32, (nd, table_rows, n), 1)
        return (all_ids[:, which][None, None] == rows_of).astype(bf16)

    base = lax.broadcasted_iota(jnp.int32, (nd, table_rows, n), 0) * table_rows
    hot_both = jnp.concatenate([hot(0, base), hot(1, base)], 1)
    embedded = jnp.einsum("sdr,srl->ld", got[:, :cols], hot_both, preferred_element_type=f32)
    condition = jax.nn.silu(embedded).astype(bf16)
    partial = dot(condition, ada_w)

    half_q = jnp.concatenate([ring_q, swap_q], 0)
    last_q = chips.swap(half_q, 1)
    block_1 = across(fc1_mine.reshape(rows, FF // 2), fc1_others.reshape(rows, FF // 2))
    block_1, swap_q = after(block_1, swap_q)
    ring_1 = jnp.concatenate(chips.ring_gather(block_1[None], True)[0], 0)
    swap_1 = chips.swap(ring_1, 0)
    half_1 = jnp.concatenate([ring_1, swap_1], 0)
    held_2, ring_1 = after(held_2, ring_1)

    lanes = 128 if (6 * D) % 128 == 0 else 6 * D
    partial = partial.reshape(n, 6 * D // lanes, lanes)
    partial = lax.all_to_all(partial, "fsdp", 0, 0, tiled=True)
    early = (fc1_bias, qv_bias, proj_bias, fc2_bias, ada_bias)
    partial, early = after(partial, early)
    fc1_bias, qv_bias, proj_bias, fc2_bias, ada_bias = early
    modulation = jnp.sum(partial, 0)
    modulation = (modulation + other_core(modulation)).reshape(6 * D) + ada_bias
    mod = modulation.reshape(6, D)

    qkv_full, proj_cols = place(chips, True, [ring_q, swap_q, last_q], [3 * half, half])
    qkv_full = qkv_full.reshape(D, 3 * half)
    proj_mine = proj_cols[: n // 2].reshape(half, half)
    proj_got = other_core(proj_cols[n // 2 :].reshape(half, half))
    (fc1_full,) = place(chips, True, [ring_1, swap_1, chips.swap(half_1, 1)], [FF // 2])
    fc1_full = fc1_full.reshape(D, FF // 2)

    all_tokens = 2 * own_tokens
    x, cot = tokens[0], tokens[1]
    wide, narrow = (all_tokens, D), (own_tokens, D)
    normed_first, qkv, attended, logs = kernel(
        attention_kernel,
        "attention",
        [(wide, bf16), ((all_tokens, 3 * half), bf16), ((all_tokens, half), bf16), ((all_tokens, 128), f32)],
        x, mod, qkv_full, qv_bias,
    )
    parts_2, attended = chips.ring_gather(held_2, False, attended)
    part, proj_full = kernel(
        project_kernel,
        "project",
        [(wide, f32), ((half, D), bf16)],
        attended, proj_mine, proj_got,
    )
    residual, branch, normed_second, activated, slope, d_mlp, fc2_grad = kernel(
        mlp_kernel,
        "mlp",
        [(wide, f32), (narrow, f32), (wide, bf16), ((all_tokens, FF // 2), bf16)]
        + [((all_tokens, FF // 2), f32), (wide, bf16), ((FF // 2, D), bf16)],
        x, part, other_core(part), proj_bias, mod, cot, fc1_full, fc1_bias,
    )
    kept_2, sent_2 = relative(chips, True, 2, [fc2_grad.reshape(n, ff_rows, D)])
    parts_2, (kept_2, sent_2) = after(parts_2, (kept_2, sent_2))
    (fc2_full,) = place(chips, False, parts_2, [D])
    fc2_full = fc2_full.reshape(FF // 2, D)
    total_2 = chips.swap_add(kept_2, sent_2, 1)

    d_pre, fc1_b_grad, part = kernel(
        mlp_back_kernel,
        "mlp_back",
        [((all_tokens, FF // 2), bf16), ((1, FF // 2), f32), (wide, f32)],
        d_mlp, slope, fc2_full, fc1_full,
    )
    got = other_core(part)
    mlp_own, mlp_sent, fc1_grad = kernel(
        mlp_grad_kernel,
        "mlp_grad",
        [(narrow, f32), (narrow, f32), ((D, FF // 2), bf16)],
        activated, fc2_full, normed_second, d_pre,
    )
    kept_1, sent_1 = relative(chips, True, 2, [fc1_grad.reshape(n, 2 * rows, FF // 2)])
    got, (kept_1, sent_1) = after(got, (kept_1, sent_1))
    total_1 = chips.swap_add(kept_1, sent_1, 1)
    d_residual, d_attended, proj_grad, proj_sent, sums_second = kernel(
        branch_back_kernel,
        "branch_back",
        [(narrow, f32), ((all_tokens, half), bf16), ((half, half), bf16), ((half, half), bf16), ((8, D), f32)],
        residual, part, got, cot, mod, branch, attended, proj_full, d_mlp,
    )
    proj_got = other_core(proj_sent)
    d_attended, total_2 = after(d_attended, total_2)
    total_2 = chips.swap_add(total_2[0], total_2[1].astype(bf16), 0)
    d_qkv, d_qkv_sum, part, sent = kernel(
        attention_back_kernel,
        "attention_back",
        [((all_tokens, 3 * half), bf16), ((1, 3 * half), f32), (narrow, f32), (narrow, f32)],
        qkv, attended, d_attended, logs, qkv_full,
    )
    got = other_core(sent)
    (qkv_grad,) = kernel(
        qkv_grad_kernel, "qkv_grad", [((D, 3 * half), bf16)], normed_first, d_qkv
    )
    blocks = (n // 2, 2 * rows, half)
    kept_q, sent_q = relative(
        chips,
        True,
        2,
        [qkv_grad.reshape(n, 2 * rows, 3 * half), proj_grad.reshape(blocks), proj_got.reshape(blocks)],
    )
    got, (kept_q, sent_q, total_2) = after(got, (kept_q, sent_q, total_2))
    total_2 = [x for half in total_2 for x in half]
    terms_2 = chips.direct_scatter(total_2)
    total_1 = chips.swap_add(total_1[0], total_1[1].astype(bf16), 0)
    mlp_got = other_core(mlp_sent)
    latents_grad, output, small = kernel(
        finish_kernel,
        "finish",
        [(narrow, f32), (narrow, bf16), ((16, D), f32)],
        part, got, latents[0], d_residual, mod, mlp_own, mlp_got, fc2_bias, residual, cot,
        sums_second, fc1_b_grad, d_qkv_sum,
    )
    total_q = chips.swap_add(kept_q, sent_q, 1)

    small = small + other_core(small)
    small, (total_q, total_1, terms_2) = after(small, (total_q, total_1, terms_2))
    total_1 = [x for half in total_1 for x in half]
    terms_1 = chips.direct_scatter(total_1)
    small = jnp.broadcast_to(small.astype(bf16)[None], (n, 16, D))
    got = lax.all_to_all(small, "fsdp", 0, 0, tiled=True)
    total_q = chips.swap_add(total_q[0], total_q[1].astype(bf16), 0)
    got, (total_q, terms_1) = after(got, (total_q, terms_1))
    total_q = [x for half in total_q for x in half]
    terms_q = chips.direct_scatter(total_q)
    ada_w_grad, d_embedded, sums = kernel(
        modulation_back_kernel,
        "modulation_back",
        [((cols, 6 * D), f32), ((cols, n), f32), ((16, D), f32)],
        got, ada_w, condition, embedded.T,
    )
    d_embedded = lax.all_to_all(
        jnp.broadcast_to(d_embedded[None], (nd, cols, n)), BOTH, 0, 0, tiled=True
    ).reshape(D, n)
    d_embedded, terms_q = after(d_embedded, terms_q)
    qkv_grad, fc1_grad, fc2_grad = (
        sum(x.astype(f32) for x in [total[0]] + terms)
        for total, terms in ((total_q, terms_q), (total_1, terms_1), (total_2, terms_2))
    )

    device = 2 * me + core
    own = device * table_rows + lax.broadcasted_iota(jnp.int32, (table_rows, n), 0)
    mask = jnp.concatenate([all_ids[:, i][None] == own for i in range(2)], 0).astype(f32)
    tables_grad = lax.dot_general(mask, d_embedded, (((1,), (1,)), ((), ())), precision=highest)

    def owned(rows_of, place, count):
        return lax.dynamic_slice(rows_of.reshape(-1), (place * count,), (count,))

    count = FF // 2 // D
    fc1_rows = lax.dynamic_slice(sums, (10 + core * count, 0), (count, D))

    def to_rows(grad):
        pair = grad.reshape(2, rows, grad.shape[1])
        mine, others = pick((pair[0], pair[1]))
        return pick((mine, other_core(others)))

    fc1_w_grad = jnp.stack(
        [x.reshape(rows, n, ff_rows) for x in to_rows(fc1_grad)], 2
    ).reshape(rows, FF)
    qp = to_rows(qkv_grad)
    proj_w_grad = jnp.concatenate([x[:, 3 * half :] for x in qp], 1)
    qkv_w_grad = jnp.stack([x[:, : 3 * half].reshape(rows, 3, half) for x in qp], 2).reshape(
        rows, 3 * D
    )
    return (
        output[None],
        latents_grad[None],
        tables_grad[:table_rows],
        tables_grad[table_rows:],
        ada_w_grad,
        owned(sums[:6], device, 6 * D // nd),
        qkv_w_grad,
        owned(sums[8:10], device, 2 * D // nd),
        proj_w_grad,
        owned(sums[6], device, rows),
        fc1_w_grad,
        owned(fc1_rows, me, ff_rows),
        fc2_grad,
        owned(sums[7], device, rows),
    )


def solution(mesh):
    assert mesh.shape["seq"] == 2
    chips = Chips(mesh.shape["fsdp"])
    tokens = P("fsdp", "seq", None)
    matrix = P(BOTH, None)
    vector = P(BOTH)
    in_specs = (
        tokens,
        P("fsdp"),
        P("fsdp"),
        matrix,
        matrix,
        matrix,
        vector,
        matrix,
        vector,
        matrix,
        vector,
        matrix,
        vector,
        matrix,
        vector,
        tokens,
    )
    out_specs = (
        tokens,
        tokens,
        matrix,
        matrix,
        matrix,
        vector,
        matrix,
        vector,
        matrix,
        vector,
        matrix,
        vector,
        matrix,
        vector,
    )
    return jax.shard_map(
        functools.partial(shards, chips),
        mesh=mesh,
        in_specs=in_specs,
        out_specs=out_specs,
        check_vma=False,
    )
```

```python
import functools

import jax
import jax.numpy as jnp
from jax import lax
from jax.experimental import pallas as pl
from jax.experimental.pallas import tpu as pltpu
from jax.sharding import PartitionSpec as P

HD = 64
norm_eps = 1e-06
highest = lax.Precision.HIGHEST
f32 = jnp.float32
bf16 = jnp.bfloat16
BOTH = ("fsdp", "seq")


def dot(a, b, out=f32):
    return jnp.dot(a, b, preferred_element_type=f32).astype(out)


def dot_t(a, b, out=f32):
    return lax.dot_general(a, b, (((0,), (0,)), ((), ())), preferred_element_type=f32).astype(out)


def dot_nt(a, b, out=f32):
    return lax.dot_general(a, b, (((1,), (1,)), ((), ())), preferred_element_type=f32).astype(out)


class Chips:
    def __init__(self, count):
        self.count = count
        self.ring = count // 4
        assert count == 4 * self.ring
        self.back = self.ring // 2
        self.ahead = self.ring - 1 - self.back
        self.offsets = [0]
        self.offsets += [-j for j in range(1, self.back + 1)]
        self.offsets += list(range(1, self.ahead + 1))

    def shift(self, x, by):
        pairs = [(i, (i + 4 * by) % self.count) for i in range(self.count)]
        with jax.named_scope(f"ring_by_{by % self.ring}"):
            return lax.ppermute(x, "fsdp", pairs)

    def swap(self, x, last):
        pairs = [
            (2 * i + core, 2 * (i ^ (1 << (core ^ last))) + core)
            for i in range(self.count)
            for core in range(2)
        ]
        with jax.named_scope("last_swap" if last else "first_swap"):
            return lax.ppermute(x, BOTH, pairs)

    def places(self, ring_first):
        me, core = lax.axis_index("fsdp"), lax.axis_index("seq")
        outer, inner = me // 4, me % 4
        places = []
        for r in range(self.count):
            swaps, place = (r // self.ring, r % self.ring) if ring_first else (r % 4, r // 4)
            a, b = swaps % 2, swaps // 2
            flip = jnp.where(core == 0, a + 2 * b, 2 * a + b)
            place = lax.rem(outer + self.offsets[place] + self.ring, self.ring)
            places.append(4 * place + jnp.bitwise_xor(inner, flip))
        return places

    def ring_gather(self, blocks, direct, tie=None):
        held = [blocks]
        if direct:
            return held + [self.shift(blocks, -offset) for offset in self.offsets[1:]], tie
        up, down = self.shift(blocks, 1), self.shift(blocks, -1)
        if tie is not None:
            up, tie = after(up, tie)
        for count, by, moved in ((self.back, 1, up), (self.ahead, -1, down)):
            for j in range(count):
                moved = self.shift(moved, by) if j else moved
                held.append(moved)
        return held, tie

    def direct_scatter(self, blocks):
        return [self.shift(x.astype(bf16), o) for x, o in zip(blocks[1:], self.offsets[1:])]

    def ring_scatter(self, blocks):
        total = blocks[0].astype(f32)
        early = []
        for first, last, by in ((self.back, 1, -1), (self.ring - 1, self.back + 1, 1)):
            term = None
            for r in range(first, last - 1, -1):
                term = blocks[r] if term is None else blocks[r].astype(f32) + term
                term = self.shift(term.astype(bf16), by)
                if r == first:
                    early.append(term)
                term = term.astype(f32)
            if term is not None:
                total = total + term
        return total, early

    def swap_add(self, kept, sent, last, count=2):
        got = self.swap(sent, last)
        size = kept.shape[0] // count
        shape = (size, *kept.shape[1:])
        outs = [(shape, bf16)] * count
        return kernel(functools.partial(add_kernel, size), "add", outs, kept, got)


def after(x, earlier):
    return lax.optimization_barrier((x, earlier))


def turned(chips, place):
    return lax.rem(place + lax.axis_index("seq") * (chips.count // 2), chips.count)


def place_kernel(chips, ring_first, sizes, widths, *refs):
    ins, outs = refs[: len(sizes)], refs[len(sizes) :]
    places = chips.places(ring_first)
    r = 0
    for ref, size in zip(ins, sizes):
        for i in range(size):
            outs[0][places[r]] = ref[i, :, : widths[0]]
            if len(outs) > 1:
                outs[1][turned(chips, places[r])] = ref[i, :, widths[0] :]
            r += 1


def add_kernel(size, kept_ref, got_ref, *outs):
    for i, out in enumerate(outs):
        for j in range(size):
            k = i * size + j
            out[j] = (kept_ref[k].astype(f32) + got_ref[k].astype(f32)).astype(out.dtype)


def relative_kernel(chips, ring_first, count, width, *refs):
    ins, outs = refs[:-count], refs[-count:]
    size, half = chips.count // count, chips.count // 2
    for r, place in enumerate(chips.places(ring_first)):
        outs[r // size][r % size, :, :width] = ins[0][place]
        if len(ins) > 1:
            at = turned(chips, place)
            low = ins[1][jnp.minimum(at, half - 1)]
            high = ins[2][jnp.maximum(at - half, 0)]
            outs[r // size][r % size, :, width:] = jnp.where(at < half, low, high)


def kernel(body, name, outs, *args, flops=0):
    shapes = [jax.ShapeDtypeStruct(shape, dtype) for shape, dtype in outs]
    moved = sum(x.size * x.dtype.itemsize for x in (*args, *shapes))
    return pl.pallas_call(
        body,
        out_shape=shapes,
        in_specs=[pl.BlockSpec(memory_space=pltpu.VMEM)] * len(args),
        out_specs=[pl.BlockSpec(memory_space=pltpu.VMEM)] * len(shapes),
        compiler_params=pltpu.CompilerParams(vmem_limit_bytes=16 << 20),
        cost_estimate=pl.CostEstimate(flops=flops, bytes_accessed=moved, transcendentals=0),
        name=name,
    )(*args)


def place(chips, ring_first, parts, widths):
    rows = parts[0].shape[1]
    if rows % 16 or any(w % 128 for w in widths):
        held = jnp.concatenate(parts, 0)
        places = jnp.stack(chips.places(ring_first))
        outs = [jnp.zeros_like(held).at[places].set(held)[:, :, : widths[0]]]
        if len(widths) > 1:
            held = held[:, :, widths[0] :]
            outs.append(jnp.zeros_like(held).at[turned(chips, places)].set(held))
        return outs
    body = functools.partial(place_kernel, chips, ring_first, [p.shape[0] for p in parts], widths)
    outs = [((chips.count, rows, w), parts[0].dtype) for w in widths]
    return kernel(body, "place", outs, *parts)


def relative(chips, ring_first, count, arrays):
    rows, width = arrays[0].shape[1:]
    widths = [a.shape[2] for a in arrays[:2]]
    if rows % 16 or any(w % 128 for w in widths):
        places = jnp.stack(chips.places(ring_first))
        held = arrays[0][places]
        if len(arrays) > 1:
            second = jnp.concatenate(arrays[1:], 0)[turned(chips, places)]
            held = jnp.concatenate([held, second], 2)
        return jnp.split(held, count)
    body = functools.partial(relative_kernel, chips, ring_first, count, width)
    shape = (chips.count // count, rows, sum(widths))
    return kernel(body, "relative", [(shape, arrays[0].dtype)] * count, *arrays)


def tiles(length, tile, body):
    def step(i, carry):
        body(pl.ds(pl.multiple_of(i * tile, tile), tile))
        return carry

    lax.fori_loop(0, length // tile, step, 0)


def normalize(v):
    center = v - jnp.mean(v, -1, keepdims=True)
    scale = lax.rsqrt(jnp.mean(center * center, -1, keepdims=True) + norm_eps)
    return center * scale, scale


def normalize_back(g, normed, scale):
    along = jnp.mean(g * normed, -1, keepdims=True)
    return scale * (g - jnp.mean(g, -1, keepdims=True) - normed * along)


def both(part, got):
    own = part.shape[0] // 2
    return part + jnp.concatenate([got[own:], got[:own]], 0)


def attention_kernel(x_ref, mod_ref, w_ref, b_ref, normed_ref, qkv_ref, att_ref, log_ref):
    normed = normalize(x_ref[...].astype(f32))[0]
    normed_ref[...] = (normed * (1.0 + mod_ref[1:2]) + mod_ref[0:1]).astype(bf16)
    half = att_ref.shape[1]
    for j in range(3):
        part = dot(normed_ref[...], w_ref[:, half * j : half * (j + 1)])
        if j != 1:
            part = part + b_ref[j // 2 : j // 2 + 1]
        qkv_ref[:, half * j : half * (j + 1)] = part.astype(bf16)
    lanes = lax.broadcasted_iota(jnp.int32, log_ref.shape, 1)
    logs = jnp.zeros(log_ref.shape, f32)
    pair = []
    for h in range(half // HD):
        q, k, v = (qkv_ref[:, half * j + HD * h : half * j + HD * (h + 1)] for j in range(3))
        scores = dot_nt(q, k) * HD ** (-0.5)
        top = jnp.max(scores, -1, keepdims=True)
        total = top + jnp.log(jnp.sum(jnp.exp(scores - top), -1, keepdims=True))
        pair.append(dot(jnp.exp(scores - total).astype(bf16), v, bf16))
        logs = jnp.where(lanes == h, total, logs)
        if h % 2:
            att_ref[:, HD * (h - 1) : HD * (h + 1)] = jnp.concatenate(pair, 1)
            pair = []
    log_ref[...] = logs


def project_kernel(att_ref, mine_ref, other_ref, part_ref, w_ref):
    half = att_ref.shape[1]
    first = lax.axis_index("seq") == 0
    w_ref[:, :half] = jnp.where(first, mine_ref[...], other_ref[...])
    w_ref[:, half:] = jnp.where(first, other_ref[...], mine_ref[...])
    part_ref[...] = dot(att_ref[...], w_ref[...])


def mlp_kernel(
    x_ref, part_ref, got_ref, bias_ref, mod_ref, cot_ref, w_ref, b_ref,
    residual_ref, branch_ref, normed_ref, act_ref, slope_ref, d_mlp_ref, grad_ref,
):
    branch = both(part_ref[...], got_ref[...]) + bias_ref[...]
    branch_ref[...] = branch[: branch_ref.shape[0]]
    residual = x_ref[...].astype(f32) + mod_ref[2:3] * branch
    residual_ref[...] = residual
    normed = normalize(residual)[0]
    normed_ref[...] = (normed * (1.0 + mod_ref[4:5]) + mod_ref[3:4]).astype(bf16)
    d_mlp_ref[...] = (cot_ref[...].astype(f32) * mod_ref[5:6]).astype(bf16)

    def tile(cols):
        v = dot(normed_ref[...], w_ref[:, cols]) + b_ref[:, cols]
        a, c = (2.0 / 3.141592653589793) ** 0.5, 0.044715
        square = v * v
        t = jnp.tanh(a * (v + c * (square * v)))
        act = (0.5 * v * (1.0 + t)).astype(bf16)
        act_ref[:, cols] = act
        slope_ref[:, cols] = 0.5 * (1.0 + t) + 0.5 * v * (1.0 - t * t) * (a * (1.0 + 3.0 * c * square))
        grad_ref[cols, :] = dot_t(act, d_mlp_ref[...], bf16)

    tiles(w_ref.shape[1], 256, tile)


def mlp_back_kernel(d_mlp_ref, slope_ref, w2_ref, w1_ref, d_pre_ref, sum_ref, d_normed_ref):
    d_normed_ref[...] = jnp.zeros_like(d_normed_ref)

    def tile(cols):
        d_pre = (dot_nt(d_mlp_ref[...], w2_ref[cols, :]) * slope_ref[:, cols]).astype(bf16)
        d_pre_ref[:, cols] = d_pre
        sum_ref[:, cols] = jnp.sum(d_pre.astype(f32), 0, keepdims=True)
        d_normed_ref[...] += dot_nt(d_pre, w1_ref[:, cols])

    tiles(w1_ref.shape[1], 256, tile)


def mlp_grad_kernel(act_ref, w2_ref, normed_ref, d_pre_ref, own_ref, sent_ref, grad_ref):
    own = own_ref.shape[0]

    def out_tile(cols):
        out = dot(act_ref[...], w2_ref[:, cols])
        own_ref[:, cols] = out[:own]
        sent_ref[:, cols] = out[own:]

    def grad_tile(cols):
        grad_ref[:, cols] = dot_t(normed_ref[...], d_pre_ref[:, cols], bf16)

    tiles(w2_ref.shape[1], 256, out_tile)
    tiles(d_pre_ref.shape[1], 256, grad_tile)


def branch_back_kernel(
    residual_ref, part_ref, got_ref, cot_ref, mod_ref, branch_ref, att_ref, w_ref, d_mlp_ref,
    d_residual_ref, d_att_ref, mine_ref, others_ref, sums_ref,
):
    own = d_residual_ref.shape[0]
    d_normed = both(part_ref[...], got_ref[...])
    normed, scale = normalize(residual_ref[...])
    back = normalize_back(d_normed * (1.0 + mod_ref[4:5]), normed, scale)
    d_residual = cot_ref[...].astype(f32) + back
    d_residual_ref[...] = d_residual[:own]
    d_branch = (d_residual * mod_ref[2:3]).astype(bf16)
    rows = (
        d_residual[:own] * branch_ref[...],
        d_normed[:own],
        d_normed[:own] * normed[:own],
        d_branch[:own].astype(f32),
        d_mlp_ref[:own, :].astype(f32),
    )
    for i, row in enumerate(rows):
        sums_ref[i : i + 1, :] = jnp.sum(row, 0, keepdims=True)
    d_att_ref[...] = dot_nt(d_branch, w_ref[...], bf16)
    grad = dot_t(att_ref[...], d_branch, bf16)
    half = mine_ref.shape[1]
    first = lax.axis_index("seq") == 0
    mine_ref[...] = jnp.where(first, grad[:, :half], grad[:, half:])
    others_ref[...] = jnp.where(first, grad[:, half:], grad[:, :half])


def attention_back_kernel(
    qkv_ref, att_ref, d_att_ref, log_ref, w_ref, d_qkv_ref, sum_ref, own_ref, sent_ref
):
    half = att_ref.shape[1]
    own = own_ref.shape[0]
    pairs = ([], [], [])
    for h in range(half // HD):
        q, k, v = (qkv_ref[:, half * j + HD * h : half * j + HD * (h + 1)] for j in range(3))
        att, d_att = (ref[:, HD * h : HD * (h + 1)] for ref in (att_ref, d_att_ref))
        exact = jnp.exp(dot_nt(q, k) * HD ** (-0.5) - log_ref[:, h : h + 1])
        delta = jnp.sum(d_att.astype(f32) * att.astype(f32), -1, keepdims=True)
        d_scores = (exact * (dot_nt(d_att, v) - delta) * HD ** (-0.5)).astype(bf16)
        pairs[0].append(dot(d_scores, k, bf16))
        pairs[1].append(dot_t(d_scores, q, bf16))
        pairs[2].append(dot_t(exact.astype(bf16), d_att, bf16))
        if h % 2:
            for j in range(3):
                cols = slice(half * j + HD * (h - 1), half * j + HD * (h + 1))
                value = jnp.concatenate(pairs[j], 1)
                d_qkv_ref[:, cols] = value
                sum_ref[:, cols] = jnp.sum(value.astype(f32), 0, keepdims=True)
            pairs = ([], [], [])

    def tile(cols):
        out = dot_nt(d_qkv_ref[...], w_ref[cols, :])
        own_ref[:, cols] = out[:own]
        sent_ref[:, cols] = out[own:]

    for start in range(0, own_ref.shape[1], 256):
        tile(slice(start, start + 256))


def qkv_grad_kernel(normed_ref, d_qkv_ref, grad_ref):
    tiles(d_qkv_ref.shape[1], 384, lambda cols: grad_ref.__setitem__(
        (slice(None), cols), dot_t(normed_ref[...], d_qkv_ref[:, cols], bf16)
    ))


def finish_kernel(
    part_ref, got_ref, x_ref, d_residual_ref, mod_ref, mlp_ref, mlp_got_ref, bias_ref, residual_ref,
    cot_ref, sums_ref, fc1_sum_ref, qkv_sum_ref, grad_ref, out_ref, small_ref,
):
    own, D = grad_ref.shape
    half = D // 2
    d_normed = part_ref[...] + got_ref[...]
    normed, scale = normalize(x_ref[...].astype(f32))
    back = normalize_back(d_normed * (1.0 + mod_ref[1:2]), normed, scale)
    grad_ref[...] = d_residual_ref[...] + back
    mlp = mlp_ref[...] + mlp_got_ref[...] + bias_ref[...]
    out_ref[...] = (residual_ref[:own, :] + mod_ref[5:6] * mlp).astype(bf16)
    first = lax.axis_index("seq") == 0
    small_ref[...] = jnp.zeros_like(small_ref)
    small_ref[0:1, :] = jnp.sum(d_normed, 0, keepdims=True)
    small_ref[1:2, :] = jnp.sum(d_normed * normed, 0, keepdims=True)
    small_ref[2:5, :] = sums_ref[0:3, :]
    small_ref[5:6, :] = jnp.sum(cot_ref[:own, :].astype(f32) * mlp, 0, keepdims=True)
    small_ref[6:8, :] = sums_ref[3:5, :]
    for i in range(2):
        part = qkv_sum_ref[:, 2 * half * i : 2 * half * i + half]
        small_ref[8 + i : 9 + i, :half] = jnp.where(first, part, 0.0)
        small_ref[8 + i : 9 + i, half:] = jnp.where(first, 0.0, part)
    count = fc1_sum_ref.shape[1] // D
    for i in range(count):
        part = fc1_sum_ref[:, D * i : D * (i + 1)]
        small_ref[10 + i : 11 + i, :] = jnp.where(first, part, 0.0)
        small_ref[10 + count + i : 11 + count + i, :] = jnp.where(first, 0.0, part)


def modulation_back_kernel(got_ref, w_ref, cond_ref, embedded_ref, grad_ref, d_embedded_ref, sums_ref):
    got = got_ref[...].astype(f32)
    sums_ref[...] = jnp.sum(got, 0)
    D = got.shape[2]
    total = jnp.zeros(d_embedded_ref.shape, f32)
    for k in range(6):
        cols = slice(D * k, D * (k + 1))
        d_mod = got[:, k].astype(bf16)
        total += dot_nt(w_ref[:, cols], d_mod)
        grad_ref[:, cols] = dot_t(cond_ref[...], d_mod)
    e = embedded_ref[...]
    gate = 1.0 / (1.0 + jnp.exp(-e))
    d_embedded_ref[...] = total * (gate * (1.0 + e * (1.0 - gate)))


def other_core(x):
    return lax.ppermute(x, "seq", [(0, 1), (1, 0)])


def shards(
    chips,
    latents,
    time_ids,
    class_ids,
    time_table,
    class_table,
    ada_w,
    ada_b,
    qkv_w,
    qv_b,
    proj_w,
    proj_b,
    fc1_w,
    fc1_b,
    fc2_w,
    fc2_b,
    cotangent,
):
    n = chips.count
    nd = 2 * n
    me, core = lax.axis_index("fsdp"), lax.axis_index("seq")
    first = core == 0
    own_tokens, D = latents.shape[1:]
    half = D // 2
    FF = fc1_w.shape[1]
    rows = qkv_w.shape[0]
    ff_rows = fc2_w.shape[0]
    table_rows = time_table.shape[0]

    def pick(pair):
        return jnp.where(first, pair[0], pair[1]), jnp.where(first, pair[1], pair[0])

    def in_order(mine, others, axis):
        a, b = pick((mine, others))
        return jnp.concatenate([a, b], axis)

    qkv_parts = qkv_w.reshape(rows, 3, 2, half)
    qkv_mine, qkv_others = pick((qkv_parts[:, :, 0], qkv_parts[:, :, 1]))
    proj_mine, proj_others = pick((proj_w[:, :half], proj_w[:, half:]))
    fc1_parts = fc1_w.reshape(rows, n, 2, ff_rows)
    fc1_mine, fc1_others = pick((fc1_parts[:, :, 0], fc1_parts[:, :, 1]))

    def across(mine, others):
        return in_order(mine, other_core(others), 0)

    block_q = across(
        jnp.concatenate([qkv_mine.reshape(rows, 3 * half), proj_mine], 1),
        jnp.concatenate([qkv_others.reshape(rows, 3 * half), proj_others], 1),
    )
    tokens = jnp.concatenate([latents, cotangent], 0)
    tokens = jnp.concatenate([tokens, other_core(tokens)], 1)

    width = 2 * table_rows
    cols = D // nd
    table = jnp.concatenate([time_table, class_table], 0).T.reshape(nd, cols, width)
    ids = jnp.stack([time_ids[0], class_ids[0]])
    ids = jnp.concatenate([ids // 32, ids % 32]).astype(bf16)
    lines, bounds = [], [cols]
    for vector in (fc1_b, qv_b, proj_b, fc2_b, ada_b, ids):
        count = -(-vector.shape[0] // width)
        lines.append(jnp.pad(vector, (0, count * width - vector.shape[0])).reshape(count, width))
        bounds.append(bounds[-1] + count)
    extras = jnp.concatenate(lines, 0)[None]
    sent = jnp.concatenate([table, jnp.broadcast_to(extras, (nd,) + extras.shape[1:])], 1)
    sent, block_q = after(sent, block_q)
    got = lax.all_to_all(sent, BOTH, 0, 0, tiled=True)

    held_2 = fc2_w[None]
    held_2 = jnp.concatenate([held_2, chips.swap(held_2, 0)], 0)
    held_2 = jnp.concatenate([held_2, chips.swap(held_2, 1)], 0)
    ring_q = jnp.concatenate(chips.ring_gather(block_q[None], True)[0], 0)
    swap_q = chips.swap(ring_q, 0)

    def extra(i, length):
        part = got[:, bounds[i] : bounds[i + 1]].reshape(nd, -1)
        return part[:, :length].astype(f32)

    fc1_bias, qv_bias, proj_bias, fc2_bias, ada_bias = (
        extra(i, b.shape[0]) for i, b in enumerate((fc1_b, qv_b, proj_b, fc2_b, ada_b))
    )
    fc1_bias = fc1_bias.reshape(n, 2, ff_rows)
    fc1_bias = pick((fc1_bias[:, 0], fc1_bias[:, 1]))[0].reshape(n * ff_rows)
    qv_bias = qv_bias.reshape(2, 2, half)
    qv_bias = pick((qv_bias[:, 0], qv_bias[:, 1]))[0]
    fc1_bias, proj_bias, fc2_bias = (x.reshape(1, -1) for x in (fc1_bias, proj_bias, fc2_bias))
    ada_bias = ada_bias.reshape(6 * D)
    id_parts = extra(5, 4)[::2].astype(jnp.int32)
    all_ids = id_parts[:, :2] * 32 + id_parts[:, 2:]

    def hot(which, base):
        rows_of = base + lax.broadcasted_iota(jnp.int32, (nd, table_rows, n), 1)
        return (all_ids[:, which][None, None] == rows_of).astype(bf16)

    base = lax.broadcasted_iota(jnp.int32, (nd, table_rows, n), 0) * table_rows
    hot_both = jnp.concatenate([hot(0, base), hot(1, base)], 1)
    embedded = jnp.einsum("sdr,srl->ld", got[:, :cols], hot_both, preferred_element_type=f32)
    condition = jax.nn.silu(embedded).astype(bf16)
    partial = dot(condition, ada_w)

    half_q = jnp.concatenate([ring_q, swap_q], 0)
    last_q = chips.swap(half_q, 1)
    block_1 = across(fc1_mine.reshape(rows, FF // 2), fc1_others.reshape(rows, FF // 2))
    block_1, ring_q = after(block_1, ring_q)
    ring_1 = jnp.concatenate(chips.ring_gather(block_1[None], True)[0], 0)
    swap_1 = chips.swap(ring_1, 0)
    half_1 = jnp.concatenate([ring_1, swap_1], 0)
    held_2, ring_1 = after(held_2, ring_1)

    lanes = 128 if (6 * D) % 128 == 0 else 6 * D
    partial = partial.reshape(n, 6 * D // lanes, lanes)
    partial = lax.all_to_all(partial, "fsdp", 0, 0, tiled=True)
    early = (fc1_bias, qv_bias, proj_bias, fc2_bias, ada_bias)
    partial, early = after(partial, early)
    fc1_bias, qv_bias, proj_bias, fc2_bias, ada_bias = early
    modulation = jnp.sum(partial, 0)
    modulation = (modulation + other_core(modulation)).reshape(6 * D) + ada_bias
    mod = modulation.reshape(6, D)

    qkv_full, proj_cols = place(chips, True, [ring_q, swap_q, last_q], [3 * half, half])
    qkv_full = qkv_full.reshape(D, 3 * half)
    proj_mine = proj_cols[: n // 2].reshape(half, half)
    proj_got = other_core(proj_cols[n // 2 :].reshape(half, half))
    (fc1_full,) = place(chips, True, [ring_1, swap_1, chips.swap(half_1, 1)], [FF // 2])
    fc1_full = fc1_full.reshape(D, FF // 2)

    all_tokens = 2 * own_tokens
    x, cot = tokens[0], tokens[1]
    wide, narrow = (all_tokens, D), (own_tokens, D)
    normed_first, qkv, attended, logs = kernel(
        attention_kernel,
        "attention",
        [(wide, bf16), ((all_tokens, 3 * half), bf16), ((all_tokens, half), bf16), ((all_tokens, 128), f32)],
        x, mod, qkv_full, qv_bias,
    )
    parts_2, attended = chips.ring_gather(held_2, False, attended)
    part, proj_full = kernel(
        project_kernel,
        "project",
        [(wide, f32), ((half, D), bf16)],
        attended, proj_mine, proj_got,
    )
    parts_2[-1], part = after(parts_2[-1], part)
    residual, branch, normed_second, activated, slope, d_mlp, fc2_grad = kernel(
        mlp_kernel,
        "mlp",
        [(wide, f32), (narrow, f32), (wide, bf16), ((all_tokens, FF // 2), bf16)]
        + [((all_tokens, FF // 2), f32), (wide, bf16), ((FF // 2, D), bf16)],
        x, part, other_core(part), proj_bias, mod, cot, fc1_full, fc1_bias,
    )
    kept_2, sent_2 = relative(chips, True, 2, [fc2_grad.reshape(n, ff_rows, D)])
    parts_2, (kept_2, sent_2) = after(parts_2, (kept_2, sent_2))
    (fc2_full,) = place(chips, False, parts_2, [D])
    fc2_full = fc2_full.reshape(FF // 2, D)
    total_2 = chips.swap_add(kept_2, sent_2, 1)

    d_pre, fc1_b_grad, part = kernel(
        mlp_back_kernel,
        "mlp_back",
        [((all_tokens, FF // 2), bf16), ((1, FF // 2), f32), (wide, f32)],
        d_mlp, slope, fc2_full, fc1_full,
    )
    got = other_core(part)
    mlp_own, mlp_sent, fc1_grad = kernel(
        mlp_grad_kernel,
        "mlp_grad",
        [(narrow, f32), (narrow, f32), ((D, FF // 2), bf16)],
        activated, fc2_full, normed_second, d_pre,
    )
    kept_1, sent_1 = relative(chips, True, 2, [fc1_grad.reshape(n, 2 * rows, FF // 2)])
    got, (kept_1, sent_1) = after(got, (kept_1, sent_1))
    total_1 = chips.swap_add(kept_1, sent_1, 1)
    d_residual, d_attended, proj_grad, proj_sent, sums_second = kernel(
        branch_back_kernel,
        "branch_back",
        [(narrow, f32), ((all_tokens, half), bf16), ((half, half), bf16), ((half, half), bf16), ((8, D), f32)],
        residual, part, got, cot, mod, branch, attended, proj_full, d_mlp,
    )
    proj_got = other_core(proj_sent)
    d_attended, total_2 = after(d_attended, total_2)
    total_2 = chips.swap_add(*total_2, 0, chips.ring)
    d_qkv, d_qkv_sum, part, sent = kernel(
        attention_back_kernel,
        "attention_back",
        [((all_tokens, 3 * half), bf16), ((1, 3 * half), f32), (narrow, f32), (narrow, f32)],
        qkv, attended, d_attended, logs, qkv_full,
    )
    got = other_core(sent)
    d_qkv, proj_got = after(d_qkv, proj_got)
    (qkv_grad,) = kernel(
        qkv_grad_kernel, "qkv_grad", [((D, 3 * half), bf16)], normed_first, d_qkv
    )
    blocks = (n // 2, 2 * rows, half)
    kept_q, sent_q = relative(
        chips,
        True,
        2,
        [qkv_grad.reshape(n, 2 * rows, 3 * half), proj_grad.reshape(blocks), proj_got.reshape(blocks)],
    )
    got, (kept_q, sent_q) = after(got, (kept_q, sent_q))
    total_1 = chips.swap_add(*total_1, 0, chips.ring)
    mlp_got = other_core(mlp_sent)
    latents_grad, output, small = kernel(
        finish_kernel,
        "finish",
        [(narrow, f32), (narrow, bf16), ((16, D), f32)],
        part, got, latents[0], d_residual, mod, mlp_own, mlp_got, fc2_bias, residual, cot,
        sums_second, fc1_b_grad, d_qkv_sum,
    )
    total_q = chips.swap_add(kept_q, sent_q, 1)

    small = small + other_core(small)
    small, total_2 = after(small, total_2)
    total_2 = [x for half in total_2 for x in half]
    terms_2 = chips.direct_scatter(total_2)
    small = jnp.broadcast_to(small.astype(bf16)[None], (n, 16, D))
    got = lax.all_to_all(small, "fsdp", 0, 0, tiled=True)
    got, (total_q, total_1, terms_2) = after(got, (total_q, total_1, terms_2))
    total_q = chips.swap_add(*total_q, 0, chips.ring)
    total_q, total_1 = ([x for half in t for x in half] for t in (total_q, total_1))
    terms_1 = chips.direct_scatter(total_1)
    ada_w_grad, d_embedded, sums = kernel(
        modulation_back_kernel,
        "modulation_back",
        [((cols, 6 * D), f32), ((cols, n), f32), ((16, D), f32)],
        got, ada_w, condition, embedded.T,
    )
    d_embedded, total_q = after(d_embedded, total_q)
    terms_q = chips.direct_scatter(total_q)
    d_embedded = lax.all_to_all(
        jnp.broadcast_to(d_embedded[None], (nd, cols, n)), BOTH, 0, 0, tiled=True
    ).reshape(D, n)
    d_embedded, (terms_q, terms_1) = after(d_embedded, (terms_q, terms_1))
    qkv_grad, fc1_grad, fc2_grad = (
        sum(x.astype(f32) for x in [total[0]] + terms)
        for total, terms in ((total_q, terms_q), (total_1, terms_1), (total_2, terms_2))
    )

    device = 2 * me + core
    own = device * table_rows + lax.broadcasted_iota(jnp.int32, (table_rows, n), 0)
    mask = jnp.concatenate([all_ids[:, i][None] == own for i in range(2)], 0).astype(f32)
    tables_grad = lax.dot_general(mask, d_embedded, (((1,), (1,)), ((), ())), precision=highest)

    def owned(rows_of, place, count):
        return lax.dynamic_slice(rows_of.reshape(-1), (place * count,), (count,))

    count = FF // 2 // D
    fc1_rows = lax.dynamic_slice(sums, (10 + core * count, 0), (count, D))

    def to_rows(grad):
        pair = grad.reshape(2, rows, grad.shape[1])
        mine, others = pick((pair[0], pair[1]))
        return pick((mine, other_core(others)))

    fc1_w_grad = jnp.stack(
        [x.reshape(rows, n, ff_rows) for x in to_rows(fc1_grad)], 2
    ).reshape(rows, FF)
    qp = to_rows(qkv_grad)
    proj_w_grad = jnp.concatenate([x[:, 3 * half :] for x in qp], 1)
    qkv_w_grad = jnp.stack([x[:, : 3 * half].reshape(rows, 3, half) for x in qp], 2).reshape(
        rows, 3 * D
    )
    return (
        output[None],
        latents_grad[None],
        tables_grad[:table_rows],
        tables_grad[table_rows:],
        ada_w_grad,
        owned(sums[:6], device, 6 * D // nd),
        qkv_w_grad,
        owned(sums[8:10], device, 2 * D // nd),
        proj_w_grad,
        owned(sums[6], device, rows),
        fc1_w_grad,
        owned(fc1_rows, me, ff_rows),
        fc2_grad,
        owned(sums[7], device, rows),
    )


def solution(mesh):
    assert mesh.shape["seq"] == 2
    chips = Chips(mesh.shape["fsdp"])
    tokens = P("fsdp", "seq", None)
    matrix = P(BOTH, None)
    vector = P(BOTH)
    in_specs = (
        tokens,
        P("fsdp"),
        P("fsdp"),
        matrix,
        matrix,
        matrix,
        vector,
        matrix,
        vector,
        matrix,
        vector,
        matrix,
        vector,
        matrix,
        vector,
        tokens,
    )
    out_specs = (
        tokens,
        tokens,
        matrix,
        matrix,
        matrix,
        vector,
        matrix,
        vector,
        matrix,
        vector,
        matrix,
        vector,
        matrix,
        vector,
    )
    return jax.shard_map(
        functools.partial(shards, chips),
        mesh=mesh,
        in_specs=in_specs,
        out_specs=out_specs,
        check_vma=False,
    )
```

```python
import functools

import jax
import jax.numpy as jnp
from jax import lax
from jax.experimental import pallas as pl
from jax.experimental.pallas import tpu as pltpu
from jax.sharding import PartitionSpec as P

HD = 64
norm_eps = 1e-06
highest = lax.Precision.HIGHEST
f32 = jnp.float32
bf16 = jnp.bfloat16
BOTH = ("fsdp", "seq")


def dot(a, b, out=f32):
    return jnp.dot(a, b, preferred_element_type=f32).astype(out)


def dot_t(a, b, out=f32):
    return lax.dot_general(a, b, (((0,), (0,)), ((), ())), preferred_element_type=f32).astype(out)


def dot_nt(a, b, out=f32):
    return lax.dot_general(a, b, (((1,), (1,)), ((), ())), preferred_element_type=f32).astype(out)


class Chips:
    def __init__(self, count):
        self.count = count
        self.ring = count // 4
        assert count == 4 * self.ring
        self.back = self.ring // 2
        self.ahead = self.ring - 1 - self.back
        self.offsets = [0]
        self.offsets += [-j for j in range(1, self.back + 1)]
        self.offsets += list(range(1, self.ahead + 1))

    def shift(self, x, by):
        pairs = [(i, (i + 4 * by) % self.count) for i in range(self.count)]
        with jax.named_scope(f"ring_by_{by % self.ring}"):
            return lax.ppermute(x, "fsdp", pairs)

    def swap(self, x, last):
        pairs = [
            (2 * i + core, 2 * (i ^ (1 << (core ^ last))) + core)
            for i in range(self.count)
            for core in range(2)
        ]
        with jax.named_scope("last_swap" if last else "first_swap"):
            return lax.ppermute(x, BOTH, pairs)

    def places(self, ring_first):
        me, core = lax.axis_index("fsdp"), lax.axis_index("seq")
        outer, inner = me // 4, me % 4
        places = []
        for r in range(self.count):
            swaps, place = (r // self.ring, r % self.ring) if ring_first else (r % 4, r // 4)
            a, b = swaps % 2, swaps // 2
            flip = jnp.where(core == 0, a + 2 * b, 2 * a + b)
            place = lax.rem(outer + self.offsets[place] + self.ring, self.ring)
            places.append(4 * place + jnp.bitwise_xor(inner, flip))
        return places

    def ring_gather(self, blocks, direct, tie=None):
        held = [blocks]
        if direct:
            return held + [self.shift(blocks, -offset) for offset in self.offsets[1:]], tie
        up, down = self.shift(blocks, 1), self.shift(blocks, -1)
        if tie is not None:
            up, tie = after(up, tie)
        for count, by, moved in ((self.back, 1, up), (self.ahead, -1, down)):
            for j in range(count):
                moved = self.shift(moved, by) if j else moved
                held.append(moved)
        return held, tie

    def direct_scatter(self, blocks):
        return [self.shift(x.astype(bf16), o) for x, o in zip(blocks[1:], self.offsets[1:])]

    def ring_scatter(self, blocks):
        total = blocks[0].astype(f32)
        early = []
        for first, last, by in ((self.back, 1, -1), (self.ring - 1, self.back + 1, 1)):
            term = None
            for r in range(first, last - 1, -1):
                term = blocks[r] if term is None else blocks[r].astype(f32) + term
                term = self.shift(term.astype(bf16), by)
                if r == first:
                    early.append(term)
                term = term.astype(f32)
            if term is not None:
                total = total + term
        return total, early

    def swap_add(self, kept, sent, last, count=2):
        got = self.swap(sent, last)
        size = kept.shape[0] // count
        shape = (size, *kept.shape[1:])
        outs = [(shape, bf16)] * count
        return kernel(functools.partial(add_kernel, size), "add", outs, kept, got)


def after(x, earlier):
    return lax.optimization_barrier((x, earlier))


def turned(chips, place):
    return lax.rem(place + lax.axis_index("seq") * (chips.count // 2), chips.count)


def place_kernel(chips, ring_first, sizes, widths, *refs):
    ins, outs = refs[: len(sizes)], refs[len(sizes) :]
    places = chips.places(ring_first)
    r = 0
    for ref, size in zip(ins, sizes):
        for i in range(size):
            outs[0][places[r]] = ref[i, :, : widths[0]]
            if len(outs) > 1:
                outs[1][turned(chips, places[r])] = ref[i, :, widths[0] :]
            r += 1


def add_kernel(size, kept_ref, got_ref, *outs):
    for i, out in enumerate(outs):
        for j in range(size):
            k = i * size + j
            out[j] = (kept_ref[k].astype(f32) + got_ref[k].astype(f32)).astype(out.dtype)


def relative_kernel(chips, ring_first, count, width, *refs):
    ins, outs = refs[:-count], refs[-count:]
    size, half = chips.count // count, chips.count // 2
    for r, place in enumerate(chips.places(ring_first)):
        outs[r // size][r % size, :, :width] = ins[0][place]
        if len(ins) > 1:
            at = turned(chips, place)
            low = ins[1][jnp.minimum(at, half - 1)]
            high = ins[2][jnp.maximum(at - half, 0)]
            outs[r // size][r % size, :, width:] = jnp.where(at < half, low, high)


def kernel(body, name, outs, *args, flops=0):
    shapes = [jax.ShapeDtypeStruct(shape, dtype) for shape, dtype in outs]
    moved = sum(x.size * x.dtype.itemsize for x in (*args, *shapes))
    return pl.pallas_call(
        body,
        out_shape=shapes,
        in_specs=[pl.BlockSpec(memory_space=pltpu.VMEM)] * len(args),
        out_specs=[pl.BlockSpec(memory_space=pltpu.VMEM)] * len(shapes),
        compiler_params=pltpu.CompilerParams(vmem_limit_bytes=16 << 20),
        cost_estimate=pl.CostEstimate(flops=flops, bytes_accessed=moved, transcendentals=0),
        name=name,
    )(*args)


def place(chips, ring_first, parts, widths):
    rows = parts[0].shape[1]
    if rows % 16 or any(w % 128 for w in widths):
        held = jnp.concatenate(parts, 0)
        places = jnp.stack(chips.places(ring_first))
        outs = [jnp.zeros_like(held).at[places].set(held)[:, :, : widths[0]]]
        if len(widths) > 1:
            held = held[:, :, widths[0] :]
            outs.append(jnp.zeros_like(held).at[turned(chips, places)].set(held))
        return outs
    body = functools.partial(place_kernel, chips, ring_first, [p.shape[0] for p in parts], widths)
    outs = [((chips.count, rows, w), parts[0].dtype) for w in widths]
    return kernel(body, "place", outs, *parts)


def relative(chips, ring_first, count, arrays):
    rows, width = arrays[0].shape[1:]
    widths = [a.shape[2] for a in arrays[:2]]
    if rows % 16 or any(w % 128 for w in widths):
        places = jnp.stack(chips.places(ring_first))
        held = arrays[0][places]
        if len(arrays) > 1:
            second = jnp.concatenate(arrays[1:], 0)[turned(chips, places)]
            held = jnp.concatenate([held, second], 2)
        return jnp.split(held, count)
    body = functools.partial(relative_kernel, chips, ring_first, count, width)
    shape = (chips.count // count, rows, sum(widths))
    return kernel(body, "relative", [(shape, arrays[0].dtype)] * count, *arrays)


def tiles(length, tile, body):
    def step(i, carry):
        body(pl.ds(pl.multiple_of(i * tile, tile), tile))
        return carry

    lax.fori_loop(0, length // tile, step, 0)


def normalize(v):
    center = v - jnp.mean(v, -1, keepdims=True)
    scale = lax.rsqrt(jnp.mean(center * center, -1, keepdims=True) + norm_eps)
    return center * scale, scale


def normalize_back(g, normed, scale):
    along = jnp.mean(g * normed, -1, keepdims=True)
    return scale * (g - jnp.mean(g, -1, keepdims=True) - normed * along)


def both(part, got):
    own = part.shape[0] // 2
    return part + jnp.concatenate([got[own:], got[:own]], 0)


def attention_kernel(x_ref, mod_ref, w_ref, b_ref, normed_ref, qkv_ref, att_ref, log_ref):
    normed = normalize(x_ref[...].astype(f32))[0]
    normed_ref[...] = (normed * (1.0 + mod_ref[1:2]) + mod_ref[0:1]).astype(bf16)
    half = att_ref.shape[1]
    for j in range(3):
        part = dot(normed_ref[...], w_ref[:, half * j : half * (j + 1)])
        if j != 1:
            part = part + b_ref[j // 2 : j // 2 + 1]
        qkv_ref[:, half * j : half * (j + 1)] = part.astype(bf16)
    lanes = lax.broadcasted_iota(jnp.int32, log_ref.shape, 1)
    logs = jnp.zeros(log_ref.shape, f32)
    pair = []
    for h in range(half // HD):
        q, k, v = (qkv_ref[:, half * j + HD * h : half * j + HD * (h + 1)] for j in range(3))
        scores = dot_nt(q, k) * HD ** (-0.5)
        top = jnp.max(scores, -1, keepdims=True)
        total = top + jnp.log(jnp.sum(jnp.exp(scores - top), -1, keepdims=True))
        pair.append(dot(jnp.exp(scores - total).astype(bf16), v, bf16))
        logs = jnp.where(lanes == h, total, logs)
        if h % 2:
            att_ref[:, HD * (h - 1) : HD * (h + 1)] = jnp.concatenate(pair, 1)
            pair = []
    log_ref[...] = logs


def project_kernel(att_ref, mine_ref, other_ref, part_ref, w_ref):
    half = att_ref.shape[1]
    first = lax.axis_index("seq") == 0
    w_ref[:, :half] = jnp.where(first, mine_ref[...], other_ref[...])
    w_ref[:, half:] = jnp.where(first, other_ref[...], mine_ref[...])
    part_ref[...] = dot(att_ref[...], w_ref[...])


def mlp_kernel(
    x_ref, part_ref, got_ref, bias_ref, mod_ref, cot_ref, w_ref, b_ref,
    residual_ref, branch_ref, normed_ref, act_ref, slope_ref, d_mlp_ref, grad_ref,
):
    branch = both(part_ref[...], got_ref[...]) + bias_ref[...]
    branch_ref[...] = branch[: branch_ref.shape[0]]
    residual = x_ref[...].astype(f32) + mod_ref[2:3] * branch
    residual_ref[...] = residual
    normed = normalize(residual)[0]
    normed_ref[...] = (normed * (1.0 + mod_ref[4:5]) + mod_ref[3:4]).astype(bf16)
    d_mlp_ref[...] = (cot_ref[...].astype(f32) * mod_ref[5:6]).astype(bf16)

    def tile(cols):
        v = dot(normed_ref[...], w_ref[:, cols]) + b_ref[:, cols]
        a, c = (2.0 / 3.141592653589793) ** 0.5, 0.044715
        square = v * v
        t = jnp.tanh(a * (v + c * (square * v)))
        act = (0.5 * v * (1.0 + t)).astype(bf16)
        act_ref[:, cols] = act
        slope_ref[:, cols] = 0.5 * (1.0 + t) + 0.5 * v * (1.0 - t * t) * (a * (1.0 + 3.0 * c * square))
        grad_ref[cols, :] = dot_t(act, d_mlp_ref[...], bf16)

    tiles(w_ref.shape[1], 512, tile)


def mlp_back_kernel(d_mlp_ref, slope_ref, w2_ref, w1_ref, d_pre_ref, sum_ref, d_normed_ref):
    d_normed_ref[...] = jnp.zeros_like(d_normed_ref)

    def tile(cols):
        d_pre = (dot_nt(d_mlp_ref[...], w2_ref[cols, :]) * slope_ref[:, cols]).astype(bf16)
        d_pre_ref[:, cols] = d_pre
        sum_ref[:, cols] = jnp.sum(d_pre.astype(f32), 0, keepdims=True)
        d_normed_ref[...] += dot_nt(d_pre, w1_ref[:, cols])

    tiles(w1_ref.shape[1], 512, tile)


def mlp_grad_kernel(act_ref, w2_ref, normed_ref, d_pre_ref, own_ref, sent_ref, grad_ref):
    own = own_ref.shape[0]

    def out_tile(cols):
        out = dot(act_ref[...], w2_ref[:, cols])
        own_ref[:, cols] = out[:own]
        sent_ref[:, cols] = out[own:]

    def grad_tile(cols):
        grad_ref[:, cols] = dot_t(normed_ref[...], d_pre_ref[:, cols], bf16)

    tiles(w2_ref.shape[1], 384, out_tile)
    tiles(d_pre_ref.shape[1], 512, grad_tile)


def branch_back_kernel(
    residual_ref, part_ref, got_ref, cot_ref, mod_ref, branch_ref, att_ref, w_ref, d_mlp_ref,
    d_residual_ref, d_att_ref, mine_ref, others_ref, sums_ref,
):
    own = d_residual_ref.shape[0]
    d_normed = both(part_ref[...], got_ref[...])
    normed, scale = normalize(residual_ref[...])
    back = normalize_back(d_normed * (1.0 + mod_ref[4:5]), normed, scale)
    d_residual = cot_ref[...].astype(f32) + back
    d_residual_ref[...] = d_residual[:own]
    d_branch = (d_residual * mod_ref[2:3]).astype(bf16)
    rows = (
        d_residual[:own] * branch_ref[...],
        d_normed[:own],
        d_normed[:own] * normed[:own],
        d_branch[:own].astype(f32),
        d_mlp_ref[:own, :].astype(f32),
    )
    for i, row in enumerate(rows):
        sums_ref[i : i + 1, :] = jnp.sum(row, 0, keepdims=True)
    d_att_ref[...] = dot_nt(d_branch, w_ref[...], bf16)
    grad = dot_t(att_ref[...], d_branch, bf16)
    half = mine_ref.shape[1]
    first = lax.axis_index("seq") == 0
    mine_ref[...] = jnp.where(first, grad[:, :half], grad[:, half:])
    others_ref[...] = jnp.where(first, grad[:, half:], grad[:, :half])


def attention_back_kernel(
    qkv_ref, att_ref, d_att_ref, log_ref, w_ref, d_qkv_ref, sum_ref, own_ref, sent_ref
):
    half = att_ref.shape[1]
    own = own_ref.shape[0]
    pairs = ([], [], [])
    for h in range(half // HD):
        q, k, v = (qkv_ref[:, half * j + HD * h : half * j + HD * (h + 1)] for j in range(3))
        att, d_att = (ref[:, HD * h : HD * (h + 1)] for ref in (att_ref, d_att_ref))
        exact = jnp.exp(dot_nt(q, k) * HD ** (-0.5) - log_ref[:, h : h + 1])
        delta = jnp.sum(d_att.astype(f32) * att.astype(f32), -1, keepdims=True)
        d_scores = (exact * (dot_nt(d_att, v) - delta) * HD ** (-0.5)).astype(bf16)
        pairs[0].append(dot(d_scores, k, bf16))
        pairs[1].append(dot_t(d_scores, q, bf16))
        pairs[2].append(dot_t(exact.astype(bf16), d_att, bf16))
        if h % 2:
            for j in range(3):
                cols = slice(half * j + HD * (h - 1), half * j + HD * (h + 1))
                value = jnp.concatenate(pairs[j], 1)
                d_qkv_ref[:, cols] = value
                sum_ref[:, cols] = jnp.sum(value.astype(f32), 0, keepdims=True)
            pairs = ([], [], [])

    def tile(cols):
        out = dot_nt(d_qkv_ref[...], w_ref[cols, :])
        own_ref[:, cols] = out[:own]
        sent_ref[:, cols] = out[own:]

    for start in range(0, own_ref.shape[1], 256):
        tile(slice(start, start + 256))


def qkv_grad_kernel(normed_ref, d_qkv_ref, grad_ref):
    tiles(d_qkv_ref.shape[1], 384, lambda cols: grad_ref.__setitem__(
        (slice(None), cols), dot_t(normed_ref[...], d_qkv_ref[:, cols], bf16)
    ))


def finish_kernel(
    part_ref, got_ref, x_ref, d_residual_ref, mod_ref, mlp_ref, mlp_got_ref, bias_ref, residual_ref,
    cot_ref, sums_ref, fc1_sum_ref, qkv_sum_ref, grad_ref, out_ref, small_ref,
):
    own, D = grad_ref.shape
    half = D // 2
    d_normed = part_ref[...] + got_ref[...]
    normed, scale = normalize(x_ref[...].astype(f32))
    back = normalize_back(d_normed * (1.0 + mod_ref[1:2]), normed, scale)
    grad_ref[...] = d_residual_ref[...] + back
    mlp = mlp_ref[...] + mlp_got_ref[...] + bias_ref[...]
    out_ref[...] = (residual_ref[:own, :] + mod_ref[5:6] * mlp).astype(bf16)
    first = lax.axis_index("seq") == 0
    small_ref[...] = jnp.zeros_like(small_ref)
    small_ref[0:1, :] = jnp.sum(d_normed, 0, keepdims=True)
    small_ref[1:2, :] = jnp.sum(d_normed * normed, 0, keepdims=True)
    small_ref[2:5, :] = sums_ref[0:3, :]
    small_ref[5:6, :] = jnp.sum(cot_ref[:own, :].astype(f32) * mlp, 0, keepdims=True)
    small_ref[6:8, :] = sums_ref[3:5, :]
    for i in range(2):
        part = qkv_sum_ref[:, 2 * half * i : 2 * half * i + half]
        small_ref[8 + i : 9 + i, :half] = jnp.where(first, part, 0.0)
        small_ref[8 + i : 9 + i, half:] = jnp.where(first, 0.0, part)
    count = fc1_sum_ref.shape[1] // D
    for i in range(count):
        part = fc1_sum_ref[:, D * i : D * (i + 1)]
        small_ref[10 + i : 11 + i, :] = jnp.where(first, part, 0.0)
        small_ref[10 + count + i : 11 + count + i, :] = jnp.where(first, 0.0, part)


def modulation_back_kernel(got_ref, w_ref, cond_ref, embedded_ref, grad_ref, d_embedded_ref, sums_ref):
    got = got_ref[...].astype(f32)
    sums_ref[...] = jnp.sum(got, 0)
    D = got.shape[2]
    total = jnp.zeros(d_embedded_ref.shape, f32)
    for k in range(6):
        cols = slice(D * k, D * (k + 1))
        d_mod = got[:, k].astype(bf16)
        total += dot_nt(w_ref[:, cols], d_mod)
        grad_ref[:, cols] = dot_t(cond_ref[...], d_mod)
    e = embedded_ref[...]
    gate = 1.0 / (1.0 + jnp.exp(-e))
    d_embedded_ref[...] = total * (gate * (1.0 + e * (1.0 - gate)))


def other_core(x):
    return lax.ppermute(x, "seq", [(0, 1), (1, 0)])


def shards(
    chips,
    latents,
    time_ids,
    class_ids,
    time_table,
    class_table,
    ada_w,
    ada_b,
    qkv_w,
    qv_b,
    proj_w,
    proj_b,
    fc1_w,
    fc1_b,
    fc2_w,
    fc2_b,
    cotangent,
):
    n = chips.count
    nd = 2 * n
    me, core = lax.axis_index("fsdp"), lax.axis_index("seq")
    first = core == 0
    own_tokens, D = latents.shape[1:]
    half = D // 2
    FF = fc1_w.shape[1]
    rows = qkv_w.shape[0]
    ff_rows = fc2_w.shape[0]
    table_rows = time_table.shape[0]

    def pick(pair):
        return jnp.where(first, pair[0], pair[1]), jnp.where(first, pair[1], pair[0])

    def in_order(mine, others, axis):
        a, b = pick((mine, others))
        return jnp.concatenate([a, b], axis)

    qkv_parts = qkv_w.reshape(rows, 3, 2, half)
    qkv_mine, qkv_others = pick((qkv_parts[:, :, 0], qkv_parts[:, :, 1]))
    proj_mine, proj_others = pick((proj_w[:, :half], proj_w[:, half:]))
    fc1_parts = fc1_w.reshape(rows, n, 2, ff_rows)
    fc1_mine, fc1_others = pick((fc1_parts[:, :, 0], fc1_parts[:, :, 1]))

    def across(mine, others):
        return in_order(mine, other_core(others), 0)

    block_q = across(
        jnp.concatenate([qkv_mine.reshape(rows, 3 * half), proj_mine], 1),
        jnp.concatenate([qkv_others.reshape(rows, 3 * half), proj_others], 1),
    )
    tokens = jnp.concatenate([latents, cotangent], 0)
    tokens = jnp.concatenate([tokens, other_core(tokens)], 1)

    width = 2 * table_rows
    cols = D // nd
    table = jnp.concatenate([time_table, class_table], 0).T.reshape(nd, cols, width)
    ids = jnp.stack([time_ids[0], class_ids[0]])
    ids = jnp.concatenate([ids // 32, ids % 32]).astype(bf16)
    lines, bounds = [], [cols]
    for vector in (fc1_b, qv_b, proj_b, fc2_b, ada_b, ids):
        count = -(-vector.shape[0] // width)
        lines.append(jnp.pad(vector, (0, count * width - vector.shape[0])).reshape(count, width))
        bounds.append(bounds[-1] + count)
    extras = jnp.concatenate(lines, 0)[None]
    sent = jnp.concatenate([table, jnp.broadcast_to(extras, (nd,) + extras.shape[1:])], 1)
    sent, block_q = after(sent, block_q)
    got = lax.all_to_all(sent, BOTH, 0, 0, tiled=True)

    held_2, block_q = after(fc2_w[None], block_q)
    held_2 = jnp.concatenate([held_2, chips.swap(held_2, 0)], 0)
    held_2 = jnp.concatenate([held_2, chips.swap(held_2, 1)], 0)
    ring_q = jnp.concatenate(chips.ring_gather(block_q[None], True)[0], 0)
    swap_q = chips.swap(ring_q, 0)

    def extra(i, length):
        part = got[:, bounds[i] : bounds[i + 1]].reshape(nd, -1)
        return part[:, :length].astype(f32)

    fc1_bias, qv_bias, proj_bias, fc2_bias, ada_bias = (
        extra(i, b.shape[0]) for i, b in enumerate((fc1_b, qv_b, proj_b, fc2_b, ada_b))
    )
    fc1_bias = fc1_bias.reshape(n, 2, ff_rows)
    fc1_bias = pick((fc1_bias[:, 0], fc1_bias[:, 1]))[0].reshape(n * ff_rows)
    qv_bias = qv_bias.reshape(2, 2, half)
    qv_bias = pick((qv_bias[:, 0], qv_bias[:, 1]))[0]
    fc1_bias, proj_bias, fc2_bias = (x.reshape(1, -1) for x in (fc1_bias, proj_bias, fc2_bias))
    ada_bias = ada_bias.reshape(6 * D)
    id_parts = extra(5, 4)[::2].astype(jnp.int32)
    all_ids = id_parts[:, :2] * 32 + id_parts[:, 2:]

    def hot(which, base):
        rows_of = base + lax.broadcasted_iota(jnp.int32, (nd, table_rows, n), 1)
        return (all_ids[:, which][None, None] == rows_of).astype(bf16)

    base = lax.broadcasted_iota(jnp.int32, (nd, table_rows, n), 0) * table_rows
    hot_both = jnp.concatenate([hot(0, base), hot(1, base)], 1)
    embedded = jnp.einsum("sdr,srl->ld", got[:, :cols], hot_both, preferred_element_type=f32)
    condition = jax.nn.silu(embedded).astype(bf16)
    partial = dot(condition, ada_w)

    half_q = jnp.concatenate([ring_q, swap_q], 0)
    last_q = chips.swap(half_q, 1)
    block_1 = across(fc1_mine.reshape(rows, FF // 2), fc1_others.reshape(rows, FF // 2))
    block_1, ring_q = after(block_1, ring_q)
    ring_1 = jnp.concatenate(chips.ring_gather(block_1[None], True)[0], 0)
    swap_1 = chips.swap(ring_1, 0)
    half_1 = jnp.concatenate([ring_1, swap_1], 0)
    held_2, ring_1 = after(held_2, ring_1)

    lanes = 128 if (6 * D) % 128 == 0 else 6 * D
    partial = partial.reshape(n, 6 * D // lanes, lanes)
    partial = lax.all_to_all(partial, "fsdp", 0, 0, tiled=True)
    early = (fc1_bias, qv_bias, proj_bias, fc2_bias, ada_bias)
    partial, early = after(partial, early)
    fc1_bias, qv_bias, proj_bias, fc2_bias, ada_bias = early
    modulation = jnp.sum(partial, 0)
    modulation = (modulation + other_core(modulation)).reshape(6 * D) + ada_bias
    mod = modulation.reshape(6, D)

    qkv_full, proj_cols = place(chips, True, [ring_q, swap_q, last_q], [3 * half, half])
    qkv_full = qkv_full.reshape(D, 3 * half)
    proj_mine = proj_cols[: n // 2].reshape(half, half)
    proj_got = other_core(proj_cols[n // 2 :].reshape(half, half))
    (fc1_full,) = place(chips, True, [ring_1, swap_1, chips.swap(half_1, 1)], [FF // 2])
    fc1_full = fc1_full.reshape(D, FF // 2)

    all_tokens = 2 * own_tokens
    x, cot = tokens[0], tokens[1]
    wide, narrow = (all_tokens, D), (own_tokens, D)
    normed_first, qkv, attended, logs = kernel(
        attention_kernel,
        "attention",
        [(wide, bf16), ((all_tokens, 3 * half), bf16), ((all_tokens, half), bf16), ((all_tokens, 128), f32)],
        x, mod, qkv_full, qv_bias,
    )
    parts_2, attended = chips.ring_gather(held_2, False, attended)
    part, proj_full = kernel(
        project_kernel,
        "project",
        [(wide, f32), ((half, D), bf16)],
        attended, proj_mine, proj_got,
    )
    parts_2[-1], part = after(parts_2[-1], part)
    residual, branch, normed_second, activated, slope, d_mlp, fc2_grad = kernel(
        mlp_kernel,
        "mlp",
        [(wide, f32), (narrow, f32), (wide, bf16), ((all_tokens, FF // 2), bf16)]
        + [((all_tokens, FF // 2), f32), (wide, bf16), ((FF // 2, D), bf16)],
        x, part, other_core(part), proj_bias, mod, cot, fc1_full, fc1_bias,
    )
    kept_2, sent_2 = relative(chips, True, 2, [fc2_grad.reshape(n, ff_rows, D)])
    parts_2, (kept_2, sent_2) = after(parts_2, (kept_2, sent_2))
    (fc2_full,) = place(chips, False, parts_2, [D])
    fc2_full = fc2_full.reshape(FF // 2, D)
    total_2 = chips.swap_add(kept_2, sent_2, 1)

    d_pre, fc1_b_grad, part = kernel(
        mlp_back_kernel,
        "mlp_back",
        [((all_tokens, FF // 2), bf16), ((1, FF // 2), f32), (wide, f32)],
        d_mlp, slope, fc2_full, fc1_full,
    )
    got = other_core(part)
    mlp_own, mlp_sent, fc1_grad = kernel(
        mlp_grad_kernel,
        "mlp_grad",
        [(narrow, f32), (narrow, f32), ((D, FF // 2), bf16)],
        activated, fc2_full, normed_second, d_pre,
    )
    kept_1, sent_1 = relative(chips, True, 2, [fc1_grad.reshape(n, 2 * rows, FF // 2)])
    got, (kept_1, sent_1) = after(got, (kept_1, sent_1))
    total_1 = chips.swap_add(kept_1, sent_1, 1)
    d_residual, d_attended, proj_grad, proj_sent, sums_second = kernel(
        branch_back_kernel,
        "branch_back",
        [(narrow, f32), ((all_tokens, half), bf16), ((half, half), bf16), ((half, half), bf16), ((8, D), f32)],
        residual, part, got, cot, mod, branch, attended, proj_full, d_mlp,
    )
    proj_got = other_core(proj_sent)
    d_attended, total_2 = after(d_attended, total_2)
    total_2 = chips.swap_add(*total_2, 0, chips.ring)
    d_qkv, d_qkv_sum, part, sent = kernel(
        attention_back_kernel,
        "attention_back",
        [((all_tokens, 3 * half), bf16), ((1, 3 * half), f32), (narrow, f32), (narrow, f32)],
        qkv, attended, d_attended, logs, qkv_full,
    )
    got = other_core(sent)
    d_qkv, proj_got = after(d_qkv, proj_got)
    (qkv_grad,) = kernel(
        qkv_grad_kernel, "qkv_grad", [((D, 3 * half), bf16)], normed_first, d_qkv
    )
    blocks = (n // 2, 2 * rows, half)
    kept_q, sent_q = relative(
        chips,
        True,
        2,
        [qkv_grad.reshape(n, 2 * rows, 3 * half), proj_grad.reshape(blocks), proj_got.reshape(blocks)],
    )
    got, (kept_q, sent_q) = after(got, (kept_q, sent_q))
    total_1 = chips.swap_add(*total_1, 0, chips.ring)
    mlp_got = other_core(mlp_sent)
    latents_grad, output, small = kernel(
        finish_kernel,
        "finish",
        [(narrow, f32), (narrow, bf16), ((16, D), f32)],
        part, got, latents[0], d_residual, mod, mlp_own, mlp_got, fc2_bias, residual, cot,
        sums_second, fc1_b_grad, d_qkv_sum,
    )
    total_q = chips.swap_add(kept_q, sent_q, 1)

    small = small + other_core(small)
    small, total_2 = after(small, total_2)
    total_2 = [x for half in total_2 for x in half]
    terms_2 = chips.direct_scatter(total_2)
    small = jnp.broadcast_to(small.astype(bf16)[None], (n, 16, D))
    got = lax.all_to_all(small, "fsdp", 0, 0, tiled=True)
    got, (total_q, total_1, terms_2[0]) = after(got, (total_q, total_1, terms_2[0]))
    total_q = chips.swap_add(*total_q, 0, chips.ring)
    total_q, total_1 = ([x for half in t for x in half] for t in (total_q, total_1))
    terms_1 = chips.direct_scatter(total_1)
    ada_w_grad, d_embedded, sums = kernel(
        modulation_back_kernel,
        "modulation_back",
        [((cols, 6 * D), f32), ((cols, n), f32), ((16, D), f32)],
        got, ada_w, condition, embedded.T,
    )
    d_embedded, (total_q, terms_2) = after(d_embedded, (total_q, terms_2))
    terms_q = chips.direct_scatter(total_q)
    d_embedded = lax.all_to_all(
        jnp.broadcast_to(d_embedded[None], (nd, cols, n)), BOTH, 0, 0, tiled=True
    ).reshape(D, n)
    d_embedded, (terms_q, terms_1) = after(d_embedded, (terms_q, terms_1))
    qkv_grad, fc1_grad, fc2_grad = (
        sum(x.astype(f32) for x in [total[0]] + terms)
        for total, terms in ((total_q, terms_q), (total_1, terms_1), (total_2, terms_2))
    )

    device = 2 * me + core
    own = device * table_rows + lax.broadcasted_iota(jnp.int32, (table_rows, n), 0)
    mask = jnp.concatenate([all_ids[:, i][None] == own for i in range(2)], 0).astype(f32)
    tables_grad = lax.dot_general(mask, d_embedded, (((1,), (1,)), ((), ())), precision=highest)

    def owned(rows_of, place, count):
        return lax.dynamic_slice(rows_of.reshape(-1), (place * count,), (count,))

    count = FF // 2 // D
    fc1_rows = lax.dynamic_slice(sums, (10 + core * count, 0), (count, D))

    def to_rows(grad):
        pair = grad.reshape(2, rows, grad.shape[1])
        mine, others = pick((pair[0], pair[1]))
        return pick((mine, other_core(others)))

    fc1_w_grad = jnp.stack(
        [x.reshape(rows, n, ff_rows) for x in to_rows(fc1_grad)], 2
    ).reshape(rows, FF)
    qp = to_rows(qkv_grad)
    proj_w_grad = jnp.concatenate([x[:, 3 * half :] for x in qp], 1)
    qkv_w_grad = jnp.stack([x[:, : 3 * half].reshape(rows, 3, half) for x in qp], 2).reshape(
        rows, 3 * D
    )
    return (
        output[None],
        latents_grad[None],
        tables_grad[:table_rows],
        tables_grad[table_rows:],
        ada_w_grad,
        owned(sums[:6], device, 6 * D // nd),
        qkv_w_grad,
        owned(sums[8:10], device, 2 * D // nd),
        proj_w_grad,
        owned(sums[6], device, rows),
        fc1_w_grad,
        owned(fc1_rows, me, ff_rows),
        fc2_grad,
        owned(sums[7], device, rows),
    )


def solution(mesh):
    assert mesh.shape["seq"] == 2
    chips = Chips(mesh.shape["fsdp"])
    tokens = P("fsdp", "seq", None)
    matrix = P(BOTH, None)
    vector = P(BOTH)
    in_specs = (
        tokens,
        P("fsdp"),
        P("fsdp"),
        matrix,
        matrix,
        matrix,
        vector,
        matrix,
        vector,
        matrix,
        vector,
        matrix,
        vector,
        matrix,
        vector,
        tokens,
    )
    out_specs = (
        tokens,
        tokens,
        matrix,
        matrix,
        matrix,
        vector,
        matrix,
        vector,
        matrix,
        vector,
        matrix,
        vector,
        matrix,
        vector,
    )
    return jax.shard_map(
        functools.partial(shards, chips),
        mesh=mesh,
        in_specs=in_specs,
        out_specs=out_specs,
        check_vma=False,
    )
```

```python
import functools

import jax
import jax.numpy as jnp
from jax import lax
from jax.experimental import pallas as pl
from jax.experimental.pallas import tpu as pltpu
from jax.sharding import PartitionSpec as P

HD = 64
norm_eps = 1e-06
highest = lax.Precision.HIGHEST
f32 = jnp.float32
bf16 = jnp.bfloat16
BOTH = ("fsdp", "seq")


def dot(a, b, out=f32):
    return jnp.dot(a, b, preferred_element_type=f32).astype(out)


def dot_t(a, b, out=f32):
    return lax.dot_general(a, b, (((0,), (0,)), ((), ())), preferred_element_type=f32).astype(out)


def dot_nt(a, b, out=f32):
    return lax.dot_general(a, b, (((1,), (1,)), ((), ())), preferred_element_type=f32).astype(out)


class Chips:
    def __init__(self, count):
        self.count = count
        self.ring = count // 4
        assert count == 4 * self.ring
        self.back = self.ring // 2
        self.ahead = self.ring - 1 - self.back
        self.offsets = [0]
        self.offsets += [-j for j in range(1, self.back + 1)]
        self.offsets += list(range(1, self.ahead + 1))

    def shift(self, x, by):
        pairs = [(i, (i + 4 * by) % self.count) for i in range(self.count)]
        with jax.named_scope(f"ring_by_{by % self.ring}"):
            return lax.ppermute(x, "fsdp", pairs)

    def swap(self, x, last):
        pairs = [
            (2 * i + core, 2 * (i ^ (1 << (core ^ last))) + core)
            for i in range(self.count)
            for core in range(2)
        ]
        with jax.named_scope("last_swap" if last else "first_swap"):
            return lax.ppermute(x, BOTH, pairs)

    def places(self, ring_first):
        me, core = lax.axis_index("fsdp"), lax.axis_index("seq")
        outer, inner = me // 4, me % 4
        places = []
        for r in range(self.count):
            swaps, place = (r // self.ring, r % self.ring) if ring_first else (r % 4, r // 4)
            a, b = swaps % 2, swaps // 2
            flip = jnp.where(core == 0, a + 2 * b, 2 * a + b)
            place = lax.rem(outer + self.offsets[place] + self.ring, self.ring)
            places.append(4 * place + jnp.bitwise_xor(inner, flip))
        return places

    def ring_gather(self, blocks, direct, tie=None):
        held = [blocks]
        if direct:
            return held + [self.shift(blocks, -offset) for offset in self.offsets[1:]], tie
        up, down = self.shift(blocks, 1), self.shift(blocks, -1)
        if tie is not None:
            up, tie = after(up, tie)
        for count, by, moved in ((self.back, 1, up), (self.ahead, -1, down)):
            for j in range(count):
                moved = self.shift(moved, by) if j else moved
                held.append(moved)
        return held, tie

    def direct_scatter(self, blocks):
        return [self.shift(x.astype(bf16), o) for x, o in zip(blocks[1:], self.offsets[1:])]

    def ring_scatter(self, blocks):
        total = blocks[0].astype(f32)
        early = []
        for first, last, by in ((self.back, 1, -1), (self.ring - 1, self.back + 1, 1)):
            term = None
            for r in range(first, last - 1, -1):
                term = blocks[r] if term is None else blocks[r].astype(f32) + term
                term = self.shift(term.astype(bf16), by)
                if r == first:
                    early.append(term)
                term = term.astype(f32)
            if term is not None:
                total = total + term
        return total, early

    def swap_add(self, kept, sent, last, count=2):
        got = self.swap(sent, last)
        size = kept.shape[0] // count
        shape = (size, *kept.shape[1:])
        outs = [(shape, bf16)] * count
        return kernel(functools.partial(add_kernel, size), "add", outs, kept, got)


def after(x, earlier):
    return lax.optimization_barrier((x, earlier))


def turned(chips, place):
    return lax.rem(place + lax.axis_index("seq") * (chips.count // 2), chips.count)


def place_kernel(chips, ring_first, sizes, widths, *refs):
    ins, outs = refs[: len(sizes)], refs[len(sizes) :]
    places = chips.places(ring_first)
    r = 0
    for ref, size in zip(ins, sizes):
        for i in range(size):
            outs[0][places[r]] = ref[i, :, : widths[0]]
            if len(outs) > 1:
                outs[1][turned(chips, places[r])] = ref[i, :, widths[0] :]
            r += 1


def add_kernel(size, kept_ref, got_ref, *outs):
    for i, out in enumerate(outs):
        for j in range(size):
            k = i * size + j
            out[j] = (kept_ref[k].astype(f32) + got_ref[k].astype(f32)).astype(out.dtype)


def relative_kernel(chips, ring_first, count, width, *refs):
    ins, outs = refs[:-count], refs[-count:]
    size, half = chips.count // count, chips.count // 2
    for r, place in enumerate(chips.places(ring_first)):
        outs[r // size][r % size, :, :width] = ins[0][place]
        if len(ins) > 1:
            at = turned(chips, place)
            low = ins[1][jnp.minimum(at, half - 1)]
            high = ins[2][jnp.maximum(at - half, 0)]
            outs[r // size][r % size, :, width:] = jnp.where(at < half, low, high)


def kernel(body, name, outs, *args, flops=0):
    shapes = [jax.ShapeDtypeStruct(shape, dtype) for shape, dtype in outs]
    moved = sum(x.size * x.dtype.itemsize for x in (*args, *shapes))
    return pl.pallas_call(
        body,
        out_shape=shapes,
        in_specs=[pl.BlockSpec(memory_space=pltpu.VMEM)] * len(args),
        out_specs=[pl.BlockSpec(memory_space=pltpu.VMEM)] * len(shapes),
        compiler_params=pltpu.CompilerParams(vmem_limit_bytes=16 << 20),
        cost_estimate=pl.CostEstimate(flops=flops, bytes_accessed=moved, transcendentals=0),
        name=name,
    )(*args)


def place(chips, ring_first, parts, widths):
    rows = parts[0].shape[1]
    if rows % 16 or any(w % 128 for w in widths):
        held = jnp.concatenate(parts, 0)
        places = jnp.stack(chips.places(ring_first))
        outs = [jnp.zeros_like(held).at[places].set(held)[:, :, : widths[0]]]
        if len(widths) > 1:
            held = held[:, :, widths[0] :]
            outs.append(jnp.zeros_like(held).at[turned(chips, places)].set(held))
        return outs
    body = functools.partial(place_kernel, chips, ring_first, [p.shape[0] for p in parts], widths)
    outs = [((chips.count, rows, w), parts[0].dtype) for w in widths]
    return kernel(body, "place", outs, *parts)


def relative(chips, ring_first, count, arrays):
    rows, width = arrays[0].shape[1:]
    widths = [a.shape[2] for a in arrays[:2]]
    if rows % 16 or any(w % 128 for w in widths):
        places = jnp.stack(chips.places(ring_first))
        held = arrays[0][places]
        if len(arrays) > 1:
            second = jnp.concatenate(arrays[1:], 0)[turned(chips, places)]
            held = jnp.concatenate([held, second], 2)
        return jnp.split(held, count)
    body = functools.partial(relative_kernel, chips, ring_first, count, width)
    shape = (chips.count // count, rows, sum(widths))
    return kernel(body, "relative", [(shape, arrays[0].dtype)] * count, *arrays)


def tiles(length, tile, body):
    def step(i, carry):
        body(pl.ds(pl.multiple_of(i * tile, tile), tile))
        return carry

    lax.fori_loop(0, length // tile, step, 0)


def normalize(v):
    center = v - jnp.mean(v, -1, keepdims=True)
    scale = lax.rsqrt(jnp.mean(center * center, -1, keepdims=True) + norm_eps)
    return center * scale, scale


def normalize_back(g, normed, scale):
    along = jnp.mean(g * normed, -1, keepdims=True)
    return scale * (g - jnp.mean(g, -1, keepdims=True) - normed * along)


def both(part, got):
    own = part.shape[0] // 2
    return part + jnp.concatenate([got[own:], got[:own]], 0)


def attention_kernel(x_ref, mod_ref, w_ref, b_ref, normed_ref, qkv_ref, att_ref, log_ref):
    normed = normalize(x_ref[...].astype(f32))[0]
    normed_ref[...] = (normed * (1.0 + mod_ref[1:2]) + mod_ref[0:1]).astype(bf16)
    half = att_ref.shape[1]
    for j in range(3):
        part = dot(normed_ref[...], w_ref[:, half * j : half * (j + 1)])
        if j != 1:
            part = part + b_ref[j // 2 : j // 2 + 1]
        qkv_ref[:, half * j : half * (j + 1)] = part.astype(bf16)
    lanes = lax.broadcasted_iota(jnp.int32, log_ref.shape, 1)
    logs = jnp.zeros(log_ref.shape, f32)
    pair = []
    for h in range(half // HD):
        q, k, v = (qkv_ref[:, half * j + HD * h : half * j + HD * (h + 1)] for j in range(3))
        scores = dot_nt(q, k) * HD ** (-0.5)
        top = jnp.max(scores, -1, keepdims=True)
        total = top + jnp.log(jnp.sum(jnp.exp(scores - top), -1, keepdims=True))
        pair.append(dot(jnp.exp(scores - total).astype(bf16), v, bf16))
        logs = jnp.where(lanes == h, total, logs)
        if h % 2:
            att_ref[:, HD * (h - 1) : HD * (h + 1)] = jnp.concatenate(pair, 1)
            pair = []
    log_ref[...] = logs


def project_kernel(att_ref, mine_ref, other_ref, part_ref, w_ref):
    half = att_ref.shape[1]
    first = lax.axis_index("seq") == 0
    w_ref[:, :half] = jnp.where(first, mine_ref[...], other_ref[...])
    w_ref[:, half:] = jnp.where(first, other_ref[...], mine_ref[...])
    part_ref[...] = dot(att_ref[...], w_ref[...])


def mlp_kernel(
    x_ref, part_ref, got_ref, bias_ref, mod_ref, cot_ref, w_ref, b_ref,
    residual_ref, branch_ref, normed_ref, act_ref, slope_ref, d_mlp_ref, grad_ref,
):
    branch = both(part_ref[...], got_ref[...]) + bias_ref[...]
    branch_ref[...] = branch[: branch_ref.shape[0]]
    residual = x_ref[...].astype(f32) + mod_ref[2:3] * branch
    residual_ref[...] = residual
    normed = normalize(residual)[0]
    normed_ref[...] = (normed * (1.0 + mod_ref[4:5]) + mod_ref[3:4]).astype(bf16)
    d_mlp_ref[...] = (cot_ref[...].astype(f32) * mod_ref[5:6]).astype(bf16)

    def tile(cols):
        v = dot(normed_ref[...], w_ref[:, cols]) + b_ref[:, cols]
        a, c = (2.0 / 3.141592653589793) ** 0.5, 0.044715
        square = v * v
        t = jnp.tanh(a * (v + c * (square * v)))
        act = (0.5 * v * (1.0 + t)).astype(bf16)
        act_ref[:, cols] = act
        slope_ref[:, cols] = 0.5 * (1.0 + t) + 0.5 * v * (1.0 - t * t) * (a * (1.0 + 3.0 * c * square))
        grad_ref[cols, :] = dot_t(act, d_mlp_ref[...], bf16)

    tiles(w_ref.shape[1], 512, tile)


def mlp_back_kernel(d_mlp_ref, slope_ref, w2_ref, w1_ref, d_pre_ref, sum_ref, d_normed_ref):
    d_normed_ref[...] = jnp.zeros_like(d_normed_ref)

    def tile(cols):
        d_pre = (dot_nt(d_mlp_ref[...], w2_ref[cols, :]) * slope_ref[:, cols]).astype(bf16)
        d_pre_ref[:, cols] = d_pre
        sum_ref[:, cols] = jnp.sum(d_pre.astype(f32), 0, keepdims=True)
        d_normed_ref[...] += dot_nt(d_pre, w1_ref[:, cols])

    tiles(w1_ref.shape[1], 512, tile)


def mlp_grad_kernel(act_ref, w2_ref, normed_ref, d_pre_ref, own_ref, sent_ref, grad_ref):
    own = own_ref.shape[0]

    def out_tile(cols):
        out = dot(act_ref[...], w2_ref[:, cols])
        own_ref[:, cols] = out[:own]
        sent_ref[:, cols] = out[own:]

    def grad_tile(cols):
        grad_ref[:, cols] = dot_t(normed_ref[...], d_pre_ref[:, cols], bf16)

    tiles(w2_ref.shape[1], 384, out_tile)
    tiles(d_pre_ref.shape[1], 512, grad_tile)


def branch_back_kernel(
    residual_ref, part_ref, got_ref, cot_ref, mod_ref, branch_ref, att_ref, w_ref, d_mlp_ref,
    d_residual_ref, d_att_ref, mine_ref, others_ref, sums_ref,
):
    own = d_residual_ref.shape[0]
    d_normed = both(part_ref[...], got_ref[...])
    normed, scale = normalize(residual_ref[...])
    back = normalize_back(d_normed * (1.0 + mod_ref[4:5]), normed, scale)
    d_residual = cot_ref[...].astype(f32) + back
    d_residual_ref[...] = d_residual[:own]
    d_branch = (d_residual * mod_ref[2:3]).astype(bf16)
    rows = (
        d_residual[:own] * branch_ref[...],
        d_normed[:own],
        d_normed[:own] * normed[:own],
        d_branch[:own].astype(f32),
        d_mlp_ref[:own, :].astype(f32),
    )
    for i, row in enumerate(rows):
        sums_ref[i : i + 1, :] = jnp.sum(row, 0, keepdims=True)
    d_att_ref[...] = dot_nt(d_branch, w_ref[...], bf16)
    grad = dot_t(att_ref[...], d_branch, bf16)
    half = mine_ref.shape[1]
    first = lax.axis_index("seq") == 0
    mine_ref[...] = jnp.where(first, grad[:, :half], grad[:, half:])
    others_ref[...] = jnp.where(first, grad[:, half:], grad[:, :half])


def attention_back_kernel(
    qkv_ref, att_ref, d_att_ref, log_ref, w_ref, d_qkv_ref, sum_ref, own_ref, sent_ref
):
    half = att_ref.shape[1]
    own = own_ref.shape[0]
    pairs = ([], [], [])
    for h in range(half // HD):
        q, k, v = (qkv_ref[:, half * j + HD * h : half * j + HD * (h + 1)] for j in range(3))
        att, d_att = (ref[:, HD * h : HD * (h + 1)] for ref in (att_ref, d_att_ref))
        exact = jnp.exp(dot_nt(q, k) * HD ** (-0.5) - log_ref[:, h : h + 1])
        delta = jnp.sum(d_att.astype(f32) * att.astype(f32), -1, keepdims=True)
        d_scores = (exact * (dot_nt(d_att, v) - delta) * HD ** (-0.5)).astype(bf16)
        pairs[0].append(dot(d_scores, k, bf16))
        pairs[1].append(dot_t(d_scores, q, bf16))
        pairs[2].append(dot_t(exact.astype(bf16), d_att, bf16))
        if h % 2:
            for j in range(3):
                cols = slice(half * j + HD * (h - 1), half * j + HD * (h + 1))
                value = jnp.concatenate(pairs[j], 1)
                d_qkv_ref[:, cols] = value
                sum_ref[:, cols] = jnp.sum(value.astype(f32), 0, keepdims=True)
            pairs = ([], [], [])

    def tile(cols):
        out = dot_nt(d_qkv_ref[...], w_ref[cols, :])
        own_ref[:, cols] = out[:own]
        sent_ref[:, cols] = out[own:]

    for start in range(0, own_ref.shape[1], 256):
        tile(slice(start, start + 256))


def qkv_grad_kernel(normed_ref, d_qkv_ref, grad_ref):
    tiles(d_qkv_ref.shape[1], 384, lambda cols: grad_ref.__setitem__(
        (slice(None), cols), dot_t(normed_ref[...], d_qkv_ref[:, cols], bf16)
    ))


def finish_kernel(
    part_ref, got_ref, x_ref, d_residual_ref, mod_ref, mlp_ref, mlp_got_ref, bias_ref, residual_ref,
    cot_ref, sums_ref, fc1_sum_ref, qkv_sum_ref, grad_ref, out_ref, small_ref,
):
    own, D = grad_ref.shape
    half = D // 2
    d_normed = part_ref[...] + got_ref[...]
    normed, scale = normalize(x_ref[...].astype(f32))
    back = normalize_back(d_normed * (1.0 + mod_ref[1:2]), normed, scale)
    grad_ref[...] = d_residual_ref[...] + back
    mlp = mlp_ref[...] + mlp_got_ref[...] + bias_ref[...]
    out_ref[...] = (residual_ref[:own, :] + mod_ref[5:6] * mlp).astype(bf16)
    first = lax.axis_index("seq") == 0
    small_ref[...] = jnp.zeros_like(small_ref)
    small_ref[0:1, :] = jnp.sum(d_normed, 0, keepdims=True)
    small_ref[1:2, :] = jnp.sum(d_normed * normed, 0, keepdims=True)
    small_ref[2:5, :] = sums_ref[0:3, :]
    small_ref[5:6, :] = jnp.sum(cot_ref[:own, :].astype(f32) * mlp, 0, keepdims=True)
    small_ref[6:8, :] = sums_ref[3:5, :]
    for i in range(2):
        part = qkv_sum_ref[:, 2 * half * i : 2 * half * i + half]
        small_ref[8 + i : 9 + i, :half] = jnp.where(first, part, 0.0)
        small_ref[8 + i : 9 + i, half:] = jnp.where(first, 0.0, part)
    count = fc1_sum_ref.shape[1] // D
    for i in range(count):
        part = fc1_sum_ref[:, D * i : D * (i + 1)]
        small_ref[10 + i : 11 + i, :] = jnp.where(first, part, 0.0)
        small_ref[10 + count + i : 11 + count + i, :] = jnp.where(first, 0.0, part)


def modulation_back_kernel(got_ref, w_ref, cond_ref, embedded_ref, grad_ref, d_embedded_ref, sums_ref):
    got = got_ref[...].astype(f32)
    sums_ref[...] = jnp.sum(got, 0)
    D = got.shape[2]
    total = jnp.zeros(d_embedded_ref.shape, f32)
    for k in range(6):
        cols = slice(D * k, D * (k + 1))
        d_mod = got[:, k].astype(bf16)
        total += dot_nt(w_ref[:, cols], d_mod)
        grad_ref[:, cols] = dot_t(cond_ref[...], d_mod)
    e = embedded_ref[...]
    gate = 1.0 / (1.0 + jnp.exp(-e))
    d_embedded_ref[...] = total * (gate * (1.0 + e * (1.0 - gate)))


def other_core(x):
    return lax.ppermute(x, "seq", [(0, 1), (1, 0)])


def shards(
    chips,
    latents,
    time_ids,
    class_ids,
    time_table,
    class_table,
    ada_w,
    ada_b,
    qkv_w,
    qv_b,
    proj_w,
    proj_b,
    fc1_w,
    fc1_b,
    fc2_w,
    fc2_b,
    cotangent,
):
    n = chips.count
    nd = 2 * n
    me, core = lax.axis_index("fsdp"), lax.axis_index("seq")
    first = core == 0
    own_tokens, D = latents.shape[1:]
    half = D // 2
    FF = fc1_w.shape[1]
    rows = qkv_w.shape[0]
    ff_rows = fc2_w.shape[0]
    table_rows = time_table.shape[0]

    def pick(pair):
        return jnp.where(first, pair[0], pair[1]), jnp.where(first, pair[1], pair[0])

    def in_order(mine, others, axis):
        a, b = pick((mine, others))
        return jnp.concatenate([a, b], axis)

    qkv_parts = qkv_w.reshape(rows, 3, 2, half)
    qkv_mine, qkv_others = pick((qkv_parts[:, :, 0], qkv_parts[:, :, 1]))
    proj_mine, proj_others = pick((proj_w[:, :half], proj_w[:, half:]))
    fc1_parts = fc1_w.reshape(rows, n, 2, ff_rows)
    fc1_mine, fc1_others = pick((fc1_parts[:, :, 0], fc1_parts[:, :, 1]))

    def across(mine, others):
        return in_order(mine, other_core(others), 0)

    block_q = across(
        jnp.concatenate([qkv_mine.reshape(rows, 3 * half), proj_mine], 1),
        jnp.concatenate([qkv_others.reshape(rows, 3 * half), proj_others], 1),
    )
    tokens = jnp.concatenate([latents, cotangent], 0)
    tokens = jnp.concatenate([tokens, other_core(tokens)], 1)

    width = 2 * table_rows
    cols = D // nd
    table = jnp.concatenate([time_table, class_table], 0).T.reshape(nd, cols, width)
    ids = jnp.stack([time_ids[0], class_ids[0]])
    ids = jnp.concatenate([ids // 32, ids % 32]).astype(bf16)
    lines, bounds = [], [cols]
    for vector in (fc1_b, qv_b, proj_b, fc2_b, ada_b, ids):
        count = -(-vector.shape[0] // width)
        lines.append(jnp.pad(vector, (0, count * width - vector.shape[0])).reshape(count, width))
        bounds.append(bounds[-1] + count)
    extras = jnp.concatenate(lines, 0)[None]
    sent = jnp.concatenate([table, jnp.broadcast_to(extras, (nd,) + extras.shape[1:])], 1)
    sent, block_q = after(sent, block_q)
    got = lax.all_to_all(sent, BOTH, 0, 0, tiled=True)

    held_2, block_q = after(fc2_w[None], block_q)
    held_2 = jnp.concatenate([held_2, chips.swap(held_2, 0)], 0)
    held_2 = jnp.concatenate([held_2, chips.swap(held_2, 1)], 0)
    ring_q = jnp.concatenate(chips.ring_gather(block_q[None], True)[0], 0)
    swap_q = chips.swap(ring_q, 0)

    def extra(i, length):
        part = got[:, bounds[i] : bounds[i + 1]].reshape(nd, -1)
        return part[:, :length].astype(f32)

    fc1_bias, qv_bias, proj_bias, fc2_bias, ada_bias = (
        extra(i, b.shape[0]) for i, b in enumerate((fc1_b, qv_b, proj_b, fc2_b, ada_b))
    )
    fc1_bias = fc1_bias.reshape(n, 2, ff_rows)
    fc1_bias = pick((fc1_bias[:, 0], fc1_bias[:, 1]))[0].reshape(n * ff_rows)
    qv_bias = qv_bias.reshape(2, 2, half)
    qv_bias = pick((qv_bias[:, 0], qv_bias[:, 1]))[0]
    fc1_bias, proj_bias, fc2_bias = (x.reshape(1, -1) for x in (fc1_bias, proj_bias, fc2_bias))
    ada_bias = ada_bias.reshape(6 * D)
    id_parts = extra(5, 4)[::2].astype(jnp.int32)
    all_ids = id_parts[:, :2] * 32 + id_parts[:, 2:]

    def hot(which, base):
        rows_of = base + lax.broadcasted_iota(jnp.int32, (nd, table_rows, n), 1)
        return (all_ids[:, which][None, None] == rows_of).astype(bf16)

    base = lax.broadcasted_iota(jnp.int32, (nd, table_rows, n), 0) * table_rows
    hot_both = jnp.concatenate([hot(0, base), hot(1, base)], 1)
    embedded = jnp.einsum("sdr,srl->ld", got[:, :cols], hot_both, preferred_element_type=f32)
    condition = jax.nn.silu(embedded).astype(bf16)
    partial = dot(condition, ada_w)

    half_q = jnp.concatenate([ring_q, swap_q], 0)
    last_q = chips.swap(half_q, 1)
    block_1 = across(fc1_mine.reshape(rows, FF // 2), fc1_others.reshape(rows, FF // 2))
    block_1, ring_q = after(block_1, ring_q)
    ring_1 = jnp.concatenate(chips.ring_gather(block_1[None], True)[0], 0)
    swap_1 = chips.swap(ring_1, 0)
    half_1 = jnp.concatenate([ring_1, swap_1], 0)
    held_2, ring_1 = after(held_2, ring_1)

    lanes = 128 if (6 * D) % 128 == 0 else 6 * D
    partial = partial.reshape(n, 6 * D // lanes, lanes)
    partial = lax.all_to_all(partial, "fsdp", 0, 0, tiled=True)
    early = (fc1_bias, qv_bias, proj_bias, fc2_bias, ada_bias)
    partial, early = after(partial, early)
    fc1_bias, qv_bias, proj_bias, fc2_bias, ada_bias = early
    modulation = jnp.sum(partial, 0)
    modulation = (modulation + other_core(modulation)).reshape(6 * D) + ada_bias
    mod = modulation.reshape(6, D)

    qkv_full, proj_cols = place(chips, True, [ring_q, swap_q, last_q], [3 * half, half])
    qkv_full = qkv_full.reshape(D, 3 * half)
    proj_mine = proj_cols[: n // 2].reshape(half, half)
    proj_got = other_core(proj_cols[n // 2 :].reshape(half, half))
    (fc1_full,) = place(chips, True, [ring_1, swap_1, chips.swap(half_1, 1)], [FF // 2])
    fc1_full = fc1_full.reshape(D, FF // 2)

    all_tokens = 2 * own_tokens
    x, cot = tokens[0], tokens[1]
    wide, narrow = (all_tokens, D), (own_tokens, D)
    normed_first, qkv, attended, logs = kernel(
        attention_kernel,
        "attention",
        [(wide, bf16), ((all_tokens, 3 * half), bf16), ((all_tokens, half), bf16), ((all_tokens, 128), f32)],
        x, mod, qkv_full, qv_bias,
    )
    parts_2, attended = chips.ring_gather(held_2, False, attended)
    parts_2[-1], attended = after(parts_2[-1], attended)
    part, proj_full = kernel(
        project_kernel,
        "project",
        [(wide, f32), ((half, D), bf16)],
        attended, proj_mine, proj_got,
    )
    residual, branch, normed_second, activated, slope, d_mlp, fc2_grad = kernel(
        mlp_kernel,
        "mlp",
        [(wide, f32), (narrow, f32), (wide, bf16), ((all_tokens, FF // 2), bf16)]
        + [((all_tokens, FF // 2), f32), (wide, bf16), ((FF // 2, D), bf16)],
        x, part, other_core(part), proj_bias, mod, cot, fc1_full, fc1_bias,
    )
    kept_2, sent_2 = relative(chips, True, 2, [fc2_grad.reshape(n, ff_rows, D)])
    parts_2, (kept_2, sent_2) = after(parts_2, (kept_2, sent_2))
    (fc2_full,) = place(chips, False, parts_2, [D])
    fc2_full = fc2_full.reshape(FF // 2, D)
    total_2 = chips.swap_add(kept_2, sent_2, 1)

    d_pre, fc1_b_grad, part = kernel(
        mlp_back_kernel,
        "mlp_back",
        [((all_tokens, FF // 2), bf16), ((1, FF // 2), f32), (wide, f32)],
        d_mlp, slope, fc2_full, fc1_full,
    )
    got = other_core(part)
    mlp_own, mlp_sent, fc1_grad = kernel(
        mlp_grad_kernel,
        "mlp_grad",
        [(narrow, f32), (narrow, f32), ((D, FF // 2), bf16)],
        activated, fc2_full, normed_second, d_pre,
    )
    kept_1, sent_1 = relative(chips, True, 2, [fc1_grad.reshape(n, 2 * rows, FF // 2)])
    got, (kept_1, sent_1) = after(got, (kept_1, sent_1))
    total_1 = chips.swap_add(kept_1, sent_1, 1)
    d_residual, d_attended, proj_grad, proj_sent, sums_second = kernel(
        branch_back_kernel,
        "branch_back",
        [(narrow, f32), ((all_tokens, half), bf16), ((half, half), bf16), ((half, half), bf16), ((8, D), f32)],
        residual, part, got, cot, mod, branch, attended, proj_full, d_mlp,
    )
    proj_got = other_core(proj_sent)
    d_attended, total_2 = after(d_attended, total_2)
    total_2 = chips.swap_add(*total_2, 0, chips.ring)
    d_qkv, d_qkv_sum, part, sent = kernel(
        attention_back_kernel,
        "attention_back",
        [((all_tokens, 3 * half), bf16), ((1, 3 * half), f32), (narrow, f32), (narrow, f32)],
        qkv, attended, d_attended, logs, qkv_full,
    )
    got = other_core(sent)
    d_qkv, proj_got = after(d_qkv, proj_got)
    (qkv_grad,) = kernel(
        qkv_grad_kernel, "qkv_grad", [((D, 3 * half), bf16)], normed_first, d_qkv
    )
    blocks = (n // 2, 2 * rows, half)
    kept_q, sent_q = relative(
        chips,
        True,
        2,
        [qkv_grad.reshape(n, 2 * rows, 3 * half), proj_grad.reshape(blocks), proj_got.reshape(blocks)],
    )
    got, (kept_q, sent_q) = after(got, (kept_q, sent_q))
    total_1 = chips.swap_add(*total_1, 0, chips.ring)
    mlp_got = other_core(mlp_sent)
    latents_grad, output, small = kernel(
        finish_kernel,
        "finish",
        [(narrow, f32), (narrow, bf16), ((16, D), f32)],
        part, got, latents[0], d_residual, mod, mlp_own, mlp_got, fc2_bias, residual, cot,
        sums_second, fc1_b_grad, d_qkv_sum,
    )
    total_q = chips.swap_add(kept_q, sent_q, 1)

    small = small + other_core(small)
    small, total_2 = after(small, total_2)
    total_2 = [x for half in total_2 for x in half]
    terms_2 = chips.direct_scatter(total_2)
    small = jnp.broadcast_to(small.astype(bf16)[None], (n, 16, D))
    got = lax.all_to_all(small, "fsdp", 0, 0, tiled=True)
    got, (total_q, total_1, terms_2[0]) = after(got, (total_q, total_1, terms_2[0]))
    total_q = chips.swap_add(*total_q, 0, chips.ring)
    total_q, total_1 = ([x for half in t for x in half] for t in (total_q, total_1))
    terms_1 = chips.direct_scatter(total_1)
    ada_w_grad, d_embedded, sums = kernel(
        modulation_back_kernel,
        "modulation_back",
        [((cols, 6 * D), f32), ((cols, n), f32), ((16, D), f32)],
        got, ada_w, condition, embedded.T,
    )
    d_embedded, (total_q, terms_2) = after(d_embedded, (total_q, terms_2))
    terms_q = chips.direct_scatter(total_q)
    d_embedded = lax.all_to_all(
        jnp.broadcast_to(d_embedded[None], (nd, cols, n)), BOTH, 0, 0, tiled=True
    ).reshape(D, n)
    d_embedded, (terms_q, terms_1) = after(d_embedded, (terms_q, terms_1))
    qkv_grad, fc1_grad, fc2_grad = (
        sum(x.astype(f32) for x in [total[0]] + terms)
        for total, terms in ((total_q, terms_q), (total_1, terms_1), (total_2, terms_2))
    )

    device = 2 * me + core
    own = device * table_rows + lax.broadcasted_iota(jnp.int32, (table_rows, n), 0)
    mask = jnp.concatenate([all_ids[:, i][None] == own for i in range(2)], 0).astype(f32)
    tables_grad = lax.dot_general(mask, d_embedded, (((1,), (1,)), ((), ())), precision=highest)

    def owned(rows_of, place, count):
        return lax.dynamic_slice(rows_of.reshape(-1), (place * count,), (count,))

    count = FF // 2 // D
    fc1_rows = lax.dynamic_slice(sums, (10 + core * count, 0), (count, D))

    def to_rows(grad):
        pair = grad.reshape(2, rows, grad.shape[1])
        mine, others = pick((pair[0], pair[1]))
        return pick((mine, other_core(others)))

    fc1_w_grad = jnp.stack(
        [x.reshape(rows, n, ff_rows) for x in to_rows(fc1_grad)], 2
    ).reshape(rows, FF)
    qp = to_rows(qkv_grad)
    proj_w_grad = jnp.concatenate([x[:, 3 * half :] for x in qp], 1)
    qkv_w_grad = jnp.stack([x[:, : 3 * half].reshape(rows, 3, half) for x in qp], 2).reshape(
        rows, 3 * D
    )
    return (
        output[None],
        latents_grad[None],
        tables_grad[:table_rows],
        tables_grad[table_rows:],
        ada_w_grad,
        owned(sums[:6], device, 6 * D // nd),
        qkv_w_grad,
        owned(sums[8:10], device, 2 * D // nd),
        proj_w_grad,
        owned(sums[6], device, rows),
        fc1_w_grad,
        owned(fc1_rows, me, ff_rows),
        fc2_grad,
        owned(sums[7], device, rows),
    )


def solution(mesh):
    assert mesh.shape["seq"] == 2
    chips = Chips(mesh.shape["fsdp"])
    tokens = P("fsdp", "seq", None)
    matrix = P(BOTH, None)
    vector = P(BOTH)
    in_specs = (
        tokens,
        P("fsdp"),
        P("fsdp"),
        matrix,
        matrix,
        matrix,
        vector,
        matrix,
        vector,
        matrix,
        vector,
        matrix,
        vector,
        matrix,
        vector,
        tokens,
    )
    out_specs = (
        tokens,
        tokens,
        matrix,
        matrix,
        matrix,
        vector,
        matrix,
        vector,
        matrix,
        vector,
        matrix,
        vector,
        matrix,
        vector,
    )
    return jax.shard_map(
        functools.partial(shards, chips),
        mesh=mesh,
        in_specs=in_specs,
        out_specs=out_specs,
        check_vma=False,
    )
```
